256 devices in a mesh: band: 16 (over x_lo, z), slab: 16 (over y, x_hi, core).
Axes of the slice: x: 4 (x_hi: 2, x_lo: 2; x = x_hi * 2 + x_lo), y: 4, z: 8, core: 2. Of those that a mesh axis runs over, the one named last changes fastest.
Arguments:
- orbitals: float32 [1024, 128, 512], P('band', 'slab'), may hold values from -48 to 48
- potential: float32 [128, 512], P('slab'), may hold values from -2 to 2
Outputs:
- filtered: float32 [1024, 128, 512], P('band', 'slab')
- gram_matrix: float32 [1024, 1024], P('band', 'slab')
- projected: float32 [1024, 1024], P('band', 'slab')
The draws below stay inside these ranges and needn't reach their ends.
All inputs are finite; a program needn't handle non-finite values.
Results may differ from the reference program's by a relative error of at most 0.00048.
Values may be sent and summed in bfloat16 or wider, within the bound.
No kernel may reach another device: no remote copies, remote signals or barrier semaphores. Data moves between devices by JAX's collectives and lax.ppermute only.
A program may use at most 64 MiB of HBM per device.

```python
import jax
import jax.numpy as jnp
from jax import lax

NORB = 1024
DEGREE = 4
NY = 16
NX = 32
NZ = 128
NCELLS = 65536
N_BAND = 16


def level_of(rng, shape, split, least, largest):
    level, own = 1.0, jax.random.fold_in(rng, 6)
    for dim, blocks in split:
        steps = jnp.exp(jax.random.uniform(jax.random.fold_in(own, dim), (blocks,), jnp.float32, least / len(split), largest / len(split)))
        level = level * jnp.repeat(steps, shape[dim] // blocks).reshape([-1 if axis == dim else 1 for axis in range(len(shape))])
    return level


def scatter_about(rng, extent, scale, limit, split=(), held_as=jnp.bfloat16):
    loudness = level_of(rng, extent, split, -0.22, 0.18) if split else 1.0
    array = jax.random.normal(rng, extent, jnp.float32) * scale * loudness
    return jnp.minimum(jnp.maximum(array, -limit), limit).astype(held_as)


def setup_inputs(seed: int = 0) -> dict:
    keys = jax.random.split(jax.random.key(seed), 3)
    return {
        "orbitals": scatter_about(keys[0], (NORB, NZ, NX * NY), 8.0, 48.0, ((0, 16), (1, 16)), jnp.float32),
        "potential": jnp.clip(jax.random.uniform(keys[1], (NZ, NX * NY), jnp.float32, -2.0, 2.0) * level_of(keys[1], (NZ, NX * NY), ((0, 16),), -0.4, 0.0), -2.0, 2.0),
    }


COEFFS = (-5369.0 / 1800.0, 12.0 / 7.0, -15.0 / 56.0, 10.0 / 189.0, -1.0 / 112.0, 2.0 / 1925.0, -1.0 / 16632.0)
SPACING = 0.6
LOWER = -2.0
CUTOFF = 8.0
UPPER = 32.0


def plane_terms(field):
    width = field.shape[-1]
    wide = jnp.pad(field, ((0, 0), (0, 0), (6 * NY, 6 * NY)))
    narrow = jnp.pad(field, ((0, 0), (0, 0), (6, 6)))
    column = jnp.arange(width) % NY
    total = jnp.zeros_like(field)
    for reach in range(1, 7):
        upper_mask = (column + reach < NY).astype(field.dtype)
        lower_mask = (column - reach >= 0).astype(field.dtype)
        along_x = wide[:, :, (6 + reach) * NY:(6 + reach) * NY + width] + wide[:, :, (6 - reach) * NY:(6 - reach) * NY + width]
        along_y = upper_mask * narrow[:, :, 6 + reach:6 + reach + width] + lower_mask * narrow[:, :, 6 - reach:6 - reach + width]
        total = total + COEFFS[reach] * (along_x + along_y)
    return total


def apply_field(padded, field, potential):
    depth = field.shape[1]
    total = 3.0 * COEFFS[0] * field + plane_terms(field)
    for reach in range(1, 7):
        total = total + COEFFS[reach] * (padded[:, 6 + reach:6 + reach + depth] + padded[:, 6 - reach:6 - reach + depth])
    return (-0.5 / SPACING ** 2) * total + potential[None] * field


def chebyshev(start, operate):
    half_width = (UPPER - CUTOFF) / 2.0
    center = (UPPER + CUTOFF) / 2.0
    sigma_first = half_width / (LOWER - center)
    sigma = sigma_first
    previous = start
    current = (operate(start) - center * start) * (sigma_first / half_width)
    for step in range(DEGREE - 1):
        sigma_next = 1.0 / (2.0 / sigma_first - sigma)
        following = (operate(current) - center * current) * (2.0 * sigma_next / half_width) - (sigma * sigma_next) * previous
        previous = current
        current = following
        sigma = sigma_next
    return current


def reference(orbitals, potential):
    def operate(field):
        return apply_field(jnp.pad(field, ((0, 0), (6, 6), (0, 0))), field, potential)

    def filter_block(block):
        filtered_block = chebyshev(block, operate)
        return filtered_block, operate(filtered_block)

    blocks = orbitals.reshape(N_BAND, NORB // N_BAND, NZ, NX * NY)
    filtered, applied = lax.map(filter_block, blocks)
    filtered = filtered.reshape(NORB, NZ, NX * NY)
    applied = applied.reshape(NORB, NZ, NX * NY)
    filtered_low = lax.optimization_barrier(filtered.astype(jnp.bfloat16)).astype(jnp.float32).reshape(NORB, -1)
    applied_low = lax.optimization_barrier(applied.astype(jnp.bfloat16)).astype(jnp.float32).reshape(NORB, -1)
    gram_matrix = jnp.dot(filtered_low, filtered_low.T, precision=lax.Precision.HIGHEST, preferred_element_type=jnp.float32) / NCELLS
    cross = jnp.dot(applied_low, filtered_low.T, precision=lax.Precision.HIGHEST, preferred_element_type=jnp.float32)
    projected = 0.5 * (cross + cross.T) / NCELLS
    return filtered, gram_matrix, projected
```

```python
import jax
import jax.numpy as jnp
import numpy as np
from jax import lax
from jax.experimental import pallas as pl
from jax.experimental.pallas import tpu as pltpu
from jax.sharding import PartitionSpec as P

DEGREE = 4
NY = 16
NX = 32
NZ = 128
PLANE = NX * NY
NCELLS = NZ * PLANE
SLABS = 16
DEPTH = NZ // SLABS
OWN = 4
HALF = PLANE // 2
RING = 8
PEERS = 32

COEFFS = (
    -5369.0 / 1800.0,
    12.0 / 7.0,
    -15.0 / 56.0,
    10.0 / 189.0,
    -1.0 / 112.0,
    2.0 / 1925.0,
    -1.0 / 16632.0,
)
SPACING = 0.6
LOWER = -2.0
CUTOFF = 8.0
UPPER = 32.0
KINETIC = -0.5 / SPACING**2
DIAGONAL = 3.0 * COEFFS[0] * KINETIC
BF16 = jnp.bfloat16
F32 = jnp.float32


def line_matrix(size):
    matrix = np.zeros((size, size))
    for reach in range(1, 7):
        matrix += KINETIC * COEFFS[reach] * (np.eye(size, k=reach) + np.eye(size, k=-reach))
    return matrix


def two_terms(matrix):
    high = matrix.astype(jnp.bfloat16)
    low = (matrix - high.astype(np.float64)).astype(jnp.bfloat16)
    return high, low


def stencil_matrices():
    plane = np.kron(line_matrix(NX), np.eye(NY)) + np.kron(np.eye(NX), line_matrix(NY))
    plane_high, plane_low = two_terms(plane)
    z_high, z_low = two_terms(line_matrix(NZ))
    return plane_high, plane_low, np.concatenate([z_high, z_low, z_high], axis=1)


def schedule():
    half_width = (UPPER - CUTOFF) / 2.0
    center = (UPPER + CUTOFF) / 2.0
    sigma_first = half_width / (LOWER - center)
    sigma = sigma_first
    steps = [(sigma_first / half_width, center, 0.0)]
    for _ in range(DEGREE - 1):
        sigma_next = 1.0 / (2.0 / sigma_first - sigma)
        steps.append((2.0 * sigma_next / half_width, center, sigma * sigma_next))
        sigma = sigma_next
    steps.append((1.0, 0.0, 0.0))
    return steps


def filter_kernel(x_ref, mh_ref, ml_ref, z_ref, out_ref, low_ref, app_ref,
                  field_a, field_b, pot, split, total):
    for slab in range(SLABS):
        rows = slice(slab * DEPTH, (slab + 1) * DEPTH)
        for orb in range(OWN):
            field_a[orb, rows, :] = x_ref[slab, orb]
        pot[rows, :] = x_ref[slab, OWN] + DIAGONAL

    def put_low(ref, orb, value):
        for slab in range(SLABS):
            rows = slice(slab * DEPTH, (slab + 1) * DEPTH)
            for side in range(2):
                ref[side * SLABS + slab, orb] = value[rows, side * HALF : (side + 1) * HALF].astype(BF16)

    current, previous = field_a, field_b
    steps = schedule()
    for number, (scale, center, back) in enumerate(steps):
        last = number == len(steps) - 1
        for orb in range(OWN):
            value = current[orb]
            high = value.astype(BF16)
            low = (value - high.astype(F32)).astype(BF16)
            split[0, orb * NZ : (orb + 1) * NZ, :] = high
            split[1, orb * NZ : (orb + 1) * NZ, :] = low
        total[...] = (
            jnp.dot(split[0], mh_ref[...], preferred_element_type=F32)
            + jnp.dot(split[0], ml_ref[...], preferred_element_type=F32)
            + jnp.dot(split[1], mh_ref[...], preferred_element_type=F32)
        )
        for orb in range(OWN):
            rows = slice(orb * NZ, (orb + 1) * NZ)
            stack = jnp.concatenate([split[0, rows, :], split[0, rows, :], split[1, rows, :]], axis=0)
            applied = total[rows, :] + jnp.dot(z_ref[...], stack, preferred_element_type=F32)
            value = current[orb]
            applied = applied + (pot[...] - center) * value
            if last:
                put_low(app_ref, orb, applied)
                continue
            following = scale * applied
            if number:
                following = following - back * previous[orb]
            previous[orb] = following
            if number == len(steps) - 2:
                put_low(low_ref, orb, following)
                for slab in range(SLABS):
                    out_ref[slab, orb] = following[slab * DEPTH : (slab + 1) * DEPTH, :]
        current, previous = previous, current


def run_filter(block):
    plane_high, plane_low, z_stack = stencil_matrices()
    vmem = pl.BlockSpec(memory_space=pltpu.VMEM)
    return pl.pallas_call(
        filter_kernel,
        out_shape=(
            jax.ShapeDtypeStruct((SLABS, OWN, DEPTH, PLANE), F32),
            jax.ShapeDtypeStruct((PEERS, OWN, DEPTH, HALF), BF16),
            jax.ShapeDtypeStruct((PEERS, OWN, DEPTH, HALF), BF16),
        ),
        in_specs=[vmem] * 4,
        out_specs=(vmem, vmem, vmem),
        scratch_shapes=[
            pltpu.VMEM((OWN, NZ, PLANE), F32),
            pltpu.VMEM((OWN, NZ, PLANE), F32),
            pltpu.VMEM((NZ, PLANE), F32),
            pltpu.VMEM((2, OWN * NZ, PLANE), BF16),
            pltpu.VMEM((OWN * NZ, PLANE), F32),
        ],
        compiler_params=pltpu.CompilerParams(vmem_limit_bytes=40 * 1024 * 1024),
        cost_estimate=pl.CostEstimate(flops=6_000_000_000, bytes_accessed=6_000_000, transcendentals=0),
        name="chebyshev",
    )(block, jnp.asarray(plane_high), jnp.asarray(plane_low), jnp.asarray(z_stack))


def pair_kernel(w_ref, r_ref, out_ref):
    for ring in range(RING):
        part = jnp.zeros((2 * 64, 256), F32)
        for depth in range(DEPTH):
            part = part + lax.dot_general(
                r_ref[ring, depth], w_ref[depth], (((1,), (1,)), ((), ())), preferred_element_type=F32
            )
        for side in range(2):
            for own in range(2):
                out_ref[own * SLABS + side * RING + ring] = part[
                    side * 64 : (side + 1) * 64, own * 128 : (own + 1) * 128
                ]


def run_pairs(weights, gathered):
    vmem = pl.BlockSpec(memory_space=pltpu.VMEM)
    return pl.pallas_call(
        pair_kernel,
        out_shape=jax.ShapeDtypeStruct((PEERS, 64, 128), F32),
        in_specs=[vmem, vmem],
        out_specs=vmem,
        compiler_params=pltpu.CompilerParams(vmem_limit_bytes=40 * 1024 * 1024),
        cost_estimate=pl.CostEstimate(flops=1_073_741_824, bytes_accessed=6_000_000, transcendentals=0),
        name="pairs",
    )(weights, gathered)


def plane_groups():
    return [[(side * RING + ring) * SLABS + slab for side in range(2) for slab in range(SLABS)] for ring in range(RING)]


def ring_groups():
    return [[side * RING + ring for ring in range(RING)] for side in range(2)]


def over_plane(block):
    return lax.all_to_all(block, ("band", "slab"), 0, 0, axis_index_groups=plane_groups(), tiled=True)


def by_depth(block):
    return block.reshape(PEERS * OWN, DEPTH, HALF).transpose(1, 0, 2)


def on_device(orbitals, potential):
    block = orbitals.reshape(SLABS, OWN, DEPTH, PLANE)
    shared = jnp.broadcast_to(potential[None, None], (SLABS, 1, DEPTH, PLANE))
    block = lax.all_to_all(jnp.concatenate([block, shared], axis=1), "slab", 0, 0, tiled=True)
    filtered, filtered_low, applied_low = run_filter(block)
    filtered_low = by_depth(over_plane(filtered_low))
    gathered = lax.all_gather(filtered_low, "band", axis=0, axis_index_groups=ring_groups())
    applied_low = by_depth(over_plane(applied_low))
    filtered = lax.all_to_all(filtered, "slab", 0, 0, tiled=True)
    weights = jnp.concatenate(
        [filtered_low[:, :64], applied_low[:, :64], filtered_low[:, 64:], applied_low[:, 64:]], axis=1
    )
    sums = over_plane(run_pairs(weights, gathered))
    sums = jnp.sum(sums, axis=0) / NCELLS
    return (
        filtered.reshape(SLABS * OWN, DEPTH, PLANE),
        sums[:, :64].T,
        sums[:, 64:].T,
    )


def solution(mesh):
    return jax.shard_map(
        on_device,
        mesh=mesh,
        in_specs=(P("band", "slab", None), P("slab", None)),
        out_specs=(P("band", "slab", None), P("band", "slab"), P("band", "slab")),
        check_vma=False,
    )
```

```python
import jax
import jax.numpy as jnp
import numpy as np
from jax import lax
from jax.experimental import pallas as pl
from jax.experimental.pallas import tpu as pltpu
from jax.sharding import PartitionSpec as P

DEGREE = 4
NY = 16
NX = 32
NZ = 128
PLANE = NX * NY
NCELLS = NZ * PLANE
SLABS = 16
DEPTH = NZ // SLABS
OWN = 4
HALF = PLANE // 2
RING = 8
PEERS = 32

COEFFS = (
    -5369.0 / 1800.0,
    12.0 / 7.0,
    -15.0 / 56.0,
    10.0 / 189.0,
    -1.0 / 112.0,
    2.0 / 1925.0,
    -1.0 / 16632.0,
)
SPACING = 0.6
LOWER = -2.0
CUTOFF = 8.0
UPPER = 32.0
KINETIC = -0.5 / SPACING**2
DIAGONAL = 3.0 * COEFFS[0] * KINETIC
BF16 = jnp.bfloat16
F32 = jnp.float32


def line_matrix(size):
    matrix = np.zeros((size, size))
    for reach in range(1, 7):
        matrix += KINETIC * COEFFS[reach] * (np.eye(size, k=reach) + np.eye(size, k=-reach))
    return matrix


def two_terms(matrix):
    high = matrix.astype(jnp.bfloat16)
    low = (matrix - high.astype(np.float64)).astype(jnp.bfloat16)
    return high, low


def stencil_matrices():
    plane = np.kron(line_matrix(NX), np.eye(NY)) + np.kron(np.eye(NX), line_matrix(NY))
    plane_high, plane_low = two_terms(plane)
    z_high, z_low = two_terms(line_matrix(NZ))
    return plane_high, plane_low, np.concatenate([z_high, z_low, z_high], axis=1)


def schedule():
    half_width = (UPPER - CUTOFF) / 2.0
    center = (UPPER + CUTOFF) / 2.0
    sigma_first = half_width / (LOWER - center)
    sigma = sigma_first
    steps = [(sigma_first / half_width, center, 0.0)]
    for _ in range(DEGREE - 1):
        sigma_next = 1.0 / (2.0 / sigma_first - sigma)
        steps.append((2.0 * sigma_next / half_width, center, sigma * sigma_next))
        sigma = sigma_next
    steps.append((1.0, 0.0, 0.0))
    return steps


def filter_kernel(x_ref, mh_ref, ml_ref, z_ref, out_ref, low_ref, app_ref,
                  field_a, field_b, pot, split, total):
    for slab in range(SLABS):
        rows = slice(slab * DEPTH, (slab + 1) * DEPTH)
        for orb in range(OWN):
            field_a[orb, rows, :] = x_ref[slab, orb]
        pot[rows, :] = x_ref[slab, OWN] + DIAGONAL

    def put_low(ref, orb, value):
        for slab in range(SLABS):
            rows = slice(slab * DEPTH, (slab + 1) * DEPTH)
            for side in range(2):
                ref[side * SLABS + slab, orb] = value[rows, side * HALF : (side + 1) * HALF].astype(BF16)

    current, previous = field_a, field_b
    steps = schedule()
    for number, (scale, center, back) in enumerate(steps):
        last = number == len(steps) - 1
        for orb in range(OWN):
            value = current[orb]
            high = value.astype(BF16)
            low = (value - high.astype(F32)).astype(BF16)
            split[0, orb * NZ : (orb + 1) * NZ, :] = high
            split[1, orb * NZ : (orb + 1) * NZ, :] = low
        total[...] = (
            jnp.dot(split[0], mh_ref[...], preferred_element_type=F32)
            + jnp.dot(split[0], ml_ref[...], preferred_element_type=F32)
            + jnp.dot(split[1], mh_ref[...], preferred_element_type=F32)
        )
        for orb in range(OWN):
            rows = slice(orb * NZ, (orb + 1) * NZ)
            stack = jnp.concatenate([split[0, rows, :], split[0, rows, :], split[1, rows, :]], axis=0)
            applied = total[rows, :] + jnp.dot(z_ref[...], stack, preferred_element_type=F32)
            value = current[orb]
            applied = applied + (pot[...] - center) * value
            if last:
                put_low(app_ref, orb, applied)
                continue
            following = scale * applied
            if number:
                following = following - back * previous[orb]
            previous[orb] = following
            if number == len(steps) - 2:
                put_low(low_ref, orb, following)
                for slab in range(SLABS):
                    out_ref[slab, orb] = following[slab * DEPTH : (slab + 1) * DEPTH, :]
        current, previous = previous, current


def run_filter(block):
    plane_high, plane_low, z_stack = stencil_matrices()
    vmem = pl.BlockSpec(memory_space=pltpu.VMEM)
    return pl.pallas_call(
        filter_kernel,
        out_shape=(
            jax.ShapeDtypeStruct((SLABS, OWN, DEPTH, PLANE), F32),
            jax.ShapeDtypeStruct((PEERS, OWN, DEPTH, HALF), BF16),
            jax.ShapeDtypeStruct((PEERS, OWN, DEPTH, HALF), BF16),
        ),
        in_specs=[vmem] * 4,
        out_specs=(vmem, vmem, vmem),
        scratch_shapes=[
            pltpu.VMEM((OWN, NZ, PLANE), F32),
            pltpu.VMEM((OWN, NZ, PLANE), F32),
            pltpu.VMEM((NZ, PLANE), F32),
            pltpu.VMEM((2, OWN * NZ, PLANE), BF16),
            pltpu.VMEM((OWN * NZ, PLANE), F32),
        ],
        compiler_params=pltpu.CompilerParams(vmem_limit_bytes=40 * 1024 * 1024),
        cost_estimate=pl.CostEstimate(flops=6_000_000_000, bytes_accessed=6_000_000, transcendentals=0),
        name="chebyshev",
    )(block, jnp.asarray(plane_high), jnp.asarray(plane_low), jnp.asarray(z_stack))


def pair_kernel(w_ref, *refs):
    blocks, keep_ref, send_ref = refs[:-2], refs[-2], refs[-1]
    place = lax.rem(lax.axis_index("band"), RING)
    core = lax.rem(lax.axis_index("slab"), 2)
    last = RING // 2
    pieces = {0: [(0, blocks[0])]}
    for step in range(1, last):
        at = 1 + 4 * (step - 1)
        pieces[-step] = [(0, blocks[at]), (last, blocks[at + 1])]
        pieces[step] = [(0, blocks[at + 2]), (last, blocks[at + 3])]
    pieces[last] = [(0, blocks[-2]), (last, blocks[-1])]
    for shift, parts in pieces.items():
        total = jnp.zeros((128, 256), F32)
        for start, ref in parts:
            for depth in range(ref.shape[0]):
                total = total + lax.dot_general(
                    ref[depth], w_ref[start + depth], (((1,), (1,)), ((), ())), preferred_element_type=F32
                )
        ring = lax.rem(place + shift + RING, RING)
        mine = lax.rem(ring, 2) == core
        slot = lax.div(ring, 2)
        for own in range(2):
            for side in range(2):
                block = total[side * 64 : (side + 1) * 64, own * 128 : (own + 1) * 128]
                index = own * RING + side * last + slot

                @pl.when(mine)
                def _():
                    keep_ref[index] = block

                @pl.when(jnp.logical_not(mine))
                def _():
                    send_ref[index] = block


def run_pairs(weights, blocks):
    vmem = pl.BlockSpec(memory_space=pltpu.VMEM)
    shape = jax.ShapeDtypeStruct((2 * RING, 64, 128), F32)
    return pl.pallas_call(
        pair_kernel,
        out_shape=(shape, shape),
        in_specs=[vmem] * (1 + len(blocks)),
        out_specs=(vmem, vmem),
        compiler_params=pltpu.CompilerParams(vmem_limit_bytes=40 * 1024 * 1024),
        cost_estimate=pl.CostEstimate(flops=1_073_741_824, bytes_accessed=6_000_000, transcendentals=0),
        name="pairs",
    )(weights, *blocks)


def finish_kernel(parts_ref, gram_ref, projected_ref):
    total = jnp.sum(parts_ref[...], axis=0) * (1.0 / NCELLS)
    turned = total.T
    gram_ref[...] = turned[:64]
    projected_ref[...] = turned[64:]


def run_finish(parts):
    vmem = pl.BlockSpec(memory_space=pltpu.VMEM)
    shape = jax.ShapeDtypeStruct((64, 64), F32)
    return pl.pallas_call(
        finish_kernel,
        out_shape=(shape, shape),
        in_specs=[vmem],
        out_specs=(vmem, vmem),
        name="finish",
    )(parts)


def plane_groups():
    return [[(side * RING + ring) * SLABS + slab for side in range(2) for slab in range(SLABS)] for ring in range(RING)]


def core_groups():
    return [
        [(side * RING + ring) * SLABS + 2 * chip + core for side in range(2) for chip in range(SLABS // 2)]
        for ring in range(RING)
        for core in range(2)
    ]


def ring_pairs(step):
    return [
        ((side * RING + ring) * SLABS + slab, (side * RING + (ring + step) % RING) * SLABS + slab)
        for side in range(2)
        for ring in range(RING)
        for slab in range(SLABS)
    ]


def core_pairs():
    return [(place, place ^ 1) for place in range(2 * RING * SLABS)]


BOTH = ("band", "slab")


def around_ring(block):
    half = RING // 2
    ahead = [block[:half], block[half:]]
    behind = list(ahead)
    blocks = [block]
    for _ in range(half - 1):
        for chunk in range(2):
            ahead[chunk] = lax.ppermute(ahead[chunk], BOTH, ring_pairs(1))
            behind[chunk] = lax.ppermute(behind[chunk], BOTH, ring_pairs(-1))
        blocks += ahead + behind
    blocks.append(lax.ppermute(ahead[0], BOTH, ring_pairs(1)))
    blocks.append(lax.ppermute(behind[1], BOTH, ring_pairs(-1)))
    return blocks


def over_plane(block):
    return lax.all_to_all(block, BOTH, 0, 0, axis_index_groups=plane_groups(), tiled=True)


def by_depth(block):
    return block.reshape(PEERS * OWN, DEPTH, HALF).transpose(1, 0, 2)


def on_device(orbitals, potential):
    block = orbitals.reshape(SLABS, OWN, DEPTH, PLANE)
    shared = jnp.broadcast_to(potential[None, None], (SLABS, 1, DEPTH, PLANE))
    block = lax.all_to_all(jnp.concatenate([block, shared], axis=1), "slab", 0, 0, tiled=True)
    filtered, filtered_low, applied_low = run_filter(block)
    filtered_low = by_depth(over_plane(filtered_low))
    blocks = around_ring(filtered_low)
    applied_low = by_depth(over_plane(applied_low))
    filtered = lax.all_to_all(filtered, "slab", 0, 0, tiled=True)
    weights = jnp.concatenate(
        [filtered_low[:, :64], applied_low[:, :64], filtered_low[:, 64:], applied_low[:, 64:]], axis=1
    )
    keep, send = run_pairs(weights, blocks)
    sums = keep + lax.ppermute(send, BOTH, core_pairs())
    sums = lax.all_to_all(sums, BOTH, 0, 0, axis_index_groups=core_groups(), tiled=True)
    gram, projected = run_finish(sums)
    return filtered.reshape(SLABS * OWN, DEPTH, PLANE), gram, projected


def solution(mesh):
    return jax.shard_map(
        on_device,
        mesh=mesh,
        in_specs=(P("band", "slab", None), P("slab", None)),
        out_specs=(P("band", "slab", None), P("band", "slab"), P("band", "slab")),
        check_vma=False,
    )
```

```python
import jax
import jax.numpy as jnp
import numpy as np
from jax import lax
from jax.experimental import pallas as pl
from jax.experimental.pallas import tpu as pltpu
from jax.sharding import PartitionSpec as P

DEGREE = 4
NY = 16
NX = 32
NZ = 128
PLANE = NX * NY
NCELLS = NZ * PLANE
SLABS = 16
DEPTH = NZ // SLABS
OWN = 4
HALF = PLANE // 2
RING = 8
PEERS = 32

COEFFS = (
    -5369.0 / 1800.0,
    12.0 / 7.0,
    -15.0 / 56.0,
    10.0 / 189.0,
    -1.0 / 112.0,
    2.0 / 1925.0,
    -1.0 / 16632.0,
)
SPACING = 0.6
LOWER = -2.0
CUTOFF = 8.0
UPPER = 32.0
KINETIC = -0.5 / SPACING**2
DIAGONAL = 3.0 * COEFFS[0] * KINETIC
BF16 = jnp.bfloat16
F32 = jnp.float32
BOTH = ("band", "slab")
KERNEL_BYTES = 16 * 1024 * 1024


def line_matrix(size):
    matrix = np.zeros((size, size))
    for reach in range(1, 7):
        matrix += KINETIC * COEFFS[reach] * (np.eye(size, k=reach) + np.eye(size, k=-reach))
    return matrix


def two_terms(matrix):
    high = matrix.astype(jnp.bfloat16)
    low = (matrix - high.astype(np.float64)).astype(jnp.bfloat16)
    return high, low


def stencil_matrices():
    plane = np.kron(line_matrix(NX), np.eye(NY)) + np.kron(np.eye(NX), line_matrix(NY))
    plane_high, plane_low = two_terms(plane)
    z_high, z_low = two_terms(line_matrix(NZ))
    return plane_high, plane_low, np.concatenate([z_high, z_low, z_high], axis=1)


def schedule():
    half_width = (UPPER - CUTOFF) / 2.0
    center = (UPPER + CUTOFF) / 2.0
    sigma_first = half_width / (LOWER - center)
    sigma = sigma_first
    steps = [(sigma_first / half_width, center, 0.0)]
    for _ in range(DEGREE - 1):
        sigma_next = 1.0 / (2.0 / sigma_first - sigma)
        steps.append((2.0 * sigma_next / half_width, center, sigma * sigma_next))
        sigma = sigma_next
    return steps


def slab_rows(slab):
    return slice(slab * DEPTH, (slab + 1) * DEPTH)


def put_low(ref, orb, value):
    for slab in range(SLABS):
        for side in range(2):
            ref[side * SLABS + slab, orb] = value[slab_rows(slab), side * HALF : (side + 1) * HALF].astype(BF16)


def filter_kernel(x_ref, mh_ref, ml_ref, z_ref, out_ref, low_ref, field_a, field_b, pot, split, total):
    for slab in range(SLABS):
        for orb in range(OWN):
            field_a[orb, slab_rows(slab), :] = x_ref[slab, orb]
        pot[slab_rows(slab), :] = x_ref[slab, OWN] + DIAGONAL

    current, previous = field_a, field_b
    steps = schedule()
    for number, (scale, center, back) in enumerate(steps):
        for orb in range(OWN):
            rows = slice(orb * NZ, (orb + 1) * NZ)
            value = current[orb]
            high = value.astype(BF16)
            split[0, rows, :] = high
            split[1, rows, :] = (value - high.astype(F32)).astype(BF16)
        total[...] = (
            jnp.dot(split[0], mh_ref[...], preferred_element_type=F32)
            + jnp.dot(split[0], ml_ref[...], preferred_element_type=F32)
            + jnp.dot(split[1], mh_ref[...], preferred_element_type=F32)
        )
        for orb in range(OWN):
            rows = slice(orb * NZ, (orb + 1) * NZ)
            stack = jnp.concatenate([split[0, rows, :], split[0, rows, :], split[1, rows, :]], axis=0)
            applied = total[rows, :] + jnp.dot(z_ref[...], stack, preferred_element_type=F32)
            following = scale * (applied + (pot[...] - center) * current[orb])
            if number:
                following = following - back * previous[orb]
            previous[orb] = following
            if number == len(steps) - 1:
                put_low(low_ref, orb, following)
                for slab in range(SLABS):
                    out_ref[slab, orb] = following[slab_rows(slab), :]
        current, previous = previous, current


def apply_kernel(x_ref, f_ref, mh_ref, ml_ref, z_ref, app_ref, rest_ref, pot, split, total, rest):
    for slab in range(SLABS):
        for orb in range(OWN):
            rows = slice(orb * NZ + slab * DEPTH, orb * NZ + (slab + 1) * DEPTH)
            total[rows, :] = f_ref[slab, orb]
        pot[slab_rows(slab), :] = x_ref[slab, OWN] + DIAGONAL
    for orb in range(OWN):
        rows = slice(orb * NZ, (orb + 1) * NZ)
        value = total[rows, :]
        high = value.astype(BF16)
        split[0, rows, :] = high
        split[1, rows, :] = (value - high.astype(F32)).astype(BF16)
    total[...] = jnp.dot(split[0], mh_ref[...], preferred_element_type=F32) + jnp.dot(
        split[0], ml_ref[...], preferred_element_type=F32
    )
    rest[...] = jnp.dot(split[1], mh_ref[...], preferred_element_type=F32)
    for orb in range(OWN):
        rows = slice(orb * NZ, (orb + 1) * NZ)
        high, low = split[0, rows, :], split[1, rows, :]
        stack = jnp.concatenate([high, high], axis=0)
        of_low = total[rows, :] + pot[...] * high.astype(F32)
        of_low = of_low + jnp.dot(z_ref[:, : 2 * NZ], stack, preferred_element_type=F32)
        of_rest = rest[rows, :] + pot[...] * low.astype(F32)
        of_rest = of_rest + jnp.dot(z_ref[:, 2 * NZ :], low, preferred_element_type=F32)
        applied_low = (of_low + of_rest).astype(BF16).astype(F32)
        middle = 0.5 * (applied_low + of_low)
        middle_high = middle.astype(BF16).astype(F32)
        put_low(app_ref, orb, middle_high)
        put_low(rest_ref, orb, middle - middle_high)


def run_filter(block):
    plane_high, plane_low, z_stack = (jnp.asarray(matrix) for matrix in stencil_matrices())
    vmem = pl.BlockSpec(memory_space=pltpu.VMEM)
    params = pltpu.CompilerParams(vmem_limit_bytes=KERNEL_BYTES)
    filtered, filtered_low = pl.pallas_call(
        filter_kernel,
        out_shape=(
            jax.ShapeDtypeStruct((SLABS, OWN, DEPTH, PLANE), F32),
            jax.ShapeDtypeStruct((PEERS, OWN, DEPTH, HALF), BF16),
        ),
        in_specs=[vmem] * 4,
        out_specs=(vmem, vmem),
        scratch_shapes=[
            pltpu.VMEM((OWN, NZ, PLANE), F32),
            pltpu.VMEM((OWN, NZ, PLANE), F32),
            pltpu.VMEM((NZ, PLANE), F32),
            pltpu.VMEM((2, OWN * NZ, PLANE), BF16),
            pltpu.VMEM((OWN * NZ, PLANE), F32),
        ],
        compiler_params=params,
        cost_estimate=pl.CostEstimate(flops=5_000_000_000, bytes_accessed=6_000_000, transcendentals=0),
        name="chebyshev",
    )(block, plane_high, plane_low, z_stack)
    applied, rest = pl.pallas_call(
        apply_kernel,
        out_shape=(jax.ShapeDtypeStruct((PEERS, OWN, DEPTH, HALF), BF16),) * 2,
        in_specs=[vmem] * 5,
        out_specs=(vmem, vmem),
        scratch_shapes=[
            pltpu.VMEM((NZ, PLANE), F32),
            pltpu.VMEM((2, OWN * NZ, PLANE), BF16),
            pltpu.VMEM((OWN * NZ, PLANE), F32),
            pltpu.VMEM((OWN * NZ, PLANE), F32),
        ],
        compiler_params=params,
        cost_estimate=pl.CostEstimate(flops=1_000_000_000, bytes_accessed=6_000_000, transcendentals=0),
        name="applied",
    )(block, filtered, plane_high, plane_low, z_stack)
    return filtered, filtered_low, applied, rest


def put_pairs(total, shift, keep_ref, send_ref):
    place = lax.rem(lax.axis_index("band"), RING)
    core = lax.rem(lax.axis_index("slab"), 2)
    ring = lax.rem(place + shift + RING, RING)
    mine = lax.rem(ring, 2) == core
    for own in range(2):
        rows = total[own * 192 : (own + 1) * 192]
        gram, cross = rows[:64], rows[64:128] + rows[128:]
        for side in range(2):
            lanes = slice(side * 64, (side + 1) * 64)
            block = jnp.concatenate([gram[:, lanes], cross[:, lanes]], axis=1)
            index = own * RING + side * (RING // 2) + lax.div(ring, 2)
            keep_ref[jnp.where(mine, index, 2 * RING)] = block
            send_ref[jnp.where(mine, 2 * RING, index)] = block


def pair_sum(w_ref, pick):
    total = None
    for depth in range(DEPTH):
        part = lax.dot_general(w_ref[depth], pick(depth), (((1,), (1,)), ((), ())), preferred_element_type=F32)
        total = part if total is None else total + part
    return total


def early_kernel(w_ref, own_ref, *refs):
    blocks, (keep_ref, send_ref) = refs[:-2], refs[-2:]
    put_pairs(pair_sum(w_ref, lambda depth: own_ref[depth]), 0, keep_ref, send_ref)
    for step in range(1, RING // 2):
        ahead, behind = blocks[2 * step - 2], blocks[2 * step - 1]
        total = pair_sum(w_ref, lambda depth: jnp.concatenate([ahead[depth], behind[depth]], axis=0))
        put_pairs(total[:, :128], -step, keep_ref, send_ref)
        put_pairs(total[:, 128:], step, keep_ref, send_ref)


def late_kernel(w_ref, ahead_ref, behind_ref, filtered_ref, keep_in, send_in, keep_ref, send_ref, out_ref, done):
    copy = pltpu.make_async_copy(filtered_ref, out_ref, done)
    copy.start()
    first = lax.rem(lax.axis_index("slab"), 2) == 0
    total = pair_sum(w_ref, lambda depth: jnp.where(first, ahead_ref[depth], behind_ref[depth]))
    put_pairs(total, RING // 2, keep_ref, send_ref)
    copy.wait()


def run_early(weights, blocks):
    vmem = pl.BlockSpec(memory_space=pltpu.VMEM)
    shape = jax.ShapeDtypeStruct((2 * RING + 1, 64, 128), F32)
    return pl.pallas_call(
        early_kernel,
        out_shape=(shape, shape),
        in_specs=[vmem] * (1 + len(blocks)),
        out_specs=(vmem, vmem),
        compiler_params=pltpu.CompilerParams(vmem_limit_bytes=KERNEL_BYTES),
        cost_estimate=pl.CostEstimate(flops=1_400_000_000, bytes_accessed=6_000_000, transcendentals=0),
        name="pairs_early",
    )(weights, *blocks)


def run_late(weights, ahead, behind, filtered, keep, send):
    vmem = pl.BlockSpec(memory_space=pltpu.VMEM)
    shape = jax.ShapeDtypeStruct(keep.shape, F32)
    return pl.pallas_call(
        late_kernel,
        out_shape=(shape, shape, jax.ShapeDtypeStruct(filtered.shape, F32)),
        in_specs=[vmem] * 6,
        out_specs=(vmem, vmem, pl.BlockSpec(memory_space=pl.ANY)),
        scratch_shapes=[pltpu.SemaphoreType.DMA],
        input_output_aliases={4: 0, 5: 1},
        compiler_params=pltpu.CompilerParams(vmem_limit_bytes=KERNEL_BYTES),
        cost_estimate=pl.CostEstimate(flops=200_000_000, bytes_accessed=4_000_000, transcendentals=0),
        name="pairs_late",
    )(weights, ahead, behind, filtered, keep, send)


def plane_groups():
    return [[(side * RING + ring) * SLABS + slab for side in range(2) for slab in range(SLABS)] for ring in range(RING)]


def core_groups():
    return [
        [(side * RING + ring) * SLABS + 2 * chip + core for side in range(2) for chip in range(SLABS // 2)]
        for ring in range(RING)
        for core in range(2)
    ]


def ring_pairs(step, cores=(0, 1)):
    return [
        ((side * RING + ring) * SLABS + slab, (side * RING + (ring + step) % RING) * SLABS + slab)
        for side in range(2)
        for ring in range(RING)
        for slab in range(SLABS)
        if slab % 2 in cores
    ]


def core_pairs():
    return [(place, place ^ 1) for place in range(2 * RING * SLABS)]


def over_plane(block):
    return lax.all_to_all(block, BOTH, 0, 0, axis_index_groups=plane_groups(), tiled=True)


def by_depth(block):
    return block.reshape(PEERS * OWN, DEPTH, HALF).transpose(1, 0, 2)


def after(value, *earlier):
    return lax.optimization_barrier((value, *earlier))[0]


def on_device(orbitals, potential):
    block = orbitals.reshape(SLABS, OWN, DEPTH, PLANE)
    shared = jnp.broadcast_to(potential[None, None], (SLABS, 1, DEPTH, PLANE))
    block = lax.all_to_all(jnp.concatenate([block, shared], axis=1), "slab", 0, 0, tiled=True)
    filtered, filtered_low, applied, rest = run_filter(block)
    own_low = by_depth(over_plane(filtered_low))
    ahead = lax.ppermute(own_low, BOTH, ring_pairs(1))
    behind = lax.ppermute(own_low, BOTH, ring_pairs(-1))
    blocks = [own_low, ahead, behind]
    applied_high = by_depth(over_plane(applied))
    applied_rest = by_depth(over_plane(after(rest, ahead, behind)))
    ahead = lax.ppermute(ahead, BOTH, ring_pairs(1))
    behind = lax.ppermute(behind, BOTH, ring_pairs(-1))
    blocks += [ahead, behind]
    filtered = lax.all_to_all(after(filtered, ahead, behind), "slab", 0, 0, tiled=True)
    ahead = lax.ppermute(ahead, BOTH, ring_pairs(1))
    behind = lax.ppermute(behind, BOTH, ring_pairs(-1))
    blocks += [ahead, behind]
    last_ahead = lax.ppermute(ahead, BOTH, ring_pairs(1, (0,)))
    last_behind = lax.ppermute(behind, BOTH, ring_pairs(-1, (1,)))
    weights = jnp.concatenate(
        [part[:, own * 64 : (own + 1) * 64] for own in range(2) for part in (own_low, applied_high, applied_rest)],
        axis=1,
    )
    keep, send = run_early(weights, blocks)
    keep, send, filtered = run_late(weights, last_ahead, last_behind, filtered, keep, send)
    sums = (keep + lax.ppermute(send, BOTH, core_pairs()))[: 2 * RING]
    sums = lax.all_to_all(sums, BOTH, 0, 0, axis_index_groups=core_groups(), tiled=True)
    sums = jnp.sum(sums, axis=0) / NCELLS
    return filtered.reshape(SLABS * OWN, DEPTH, PLANE), sums[:, :64], sums[:, 64:]


def solution(mesh):
    return jax.shard_map(
        on_device,
        mesh=mesh,
        in_specs=(P("band", "slab", None), P("slab", None)),
        out_specs=(P("band", "slab", None), P("band", "slab"), P("band", "slab")),
        check_vma=False,
    )
```

```python
import jax
import jax.numpy as jnp
import numpy as np
from jax import lax
from jax.experimental import pallas as pl
from jax.experimental.pallas import tpu as pltpu
from jax.sharding import PartitionSpec as P

DEGREE = 4
NY = 16
NX = 32
NZ = 128
PLANE = NX * NY
NCELLS = NZ * PLANE
SLABS = 16
DEPTH = NZ // SLABS
OWN = 4
HALF = PLANE // 2
RING = 8
PEERS = 32

COEFFS = (
    -5369.0 / 1800.0,
    12.0 / 7.0,
    -15.0 / 56.0,
    10.0 / 189.0,
    -1.0 / 112.0,
    2.0 / 1925.0,
    -1.0 / 16632.0,
)
SPACING = 0.6
LOWER = -2.0
CUTOFF = 8.0
UPPER = 32.0
KINETIC = -0.5 / SPACING**2
DIAGONAL = 3.0 * COEFFS[0] * KINETIC
BF16 = jnp.bfloat16
F32 = jnp.float32
BOTH = ("band", "slab")
KERNEL_BYTES = 16 * 1024 * 1024


def line_matrix(size):
    matrix = np.zeros((size, size))
    for reach in range(1, 7):
        matrix += KINETIC * COEFFS[reach] * (np.eye(size, k=reach) + np.eye(size, k=-reach))
    return matrix


def two_terms(matrix):
    high = matrix.astype(jnp.bfloat16)
    low = (matrix - high.astype(np.float64)).astype(jnp.bfloat16)
    return high, low


def stencil_matrices():
    plane = np.kron(line_matrix(NX), np.eye(NY)) + np.kron(np.eye(NX), line_matrix(NY))
    plane_high, plane_low = two_terms(plane)
    z_high, z_low = two_terms(line_matrix(NZ))
    return plane_high, plane_low, np.concatenate([z_high, z_low, z_high], axis=1)


def schedule():
    half_width = (UPPER - CUTOFF) / 2.0
    center = (UPPER + CUTOFF) / 2.0
    sigma_first = half_width / (LOWER - center)
    sigma = sigma_first
    steps = [(sigma_first / half_width, center, 0.0)]
    for _ in range(DEGREE - 1):
        sigma_next = 1.0 / (2.0 / sigma_first - sigma)
        steps.append((2.0 * sigma_next / half_width, center, sigma * sigma_next))
        sigma = sigma_next
    return steps


def slab_rows(slab):
    return slice(slab * DEPTH, (slab + 1) * DEPTH)


def put_low(ref, orb, value):
    for slab in range(SLABS):
        for side in range(2):
            ref[side * SLABS + slab, orb] = value[slab_rows(slab), side * HALF : (side + 1) * HALF].astype(BF16)


def filter_kernel(x_ref, mh_ref, ml_ref, z_ref, out_ref, low_ref, field_a, field_b, pot, split, total):
    for slab in range(SLABS):
        for orb in range(OWN):
            field_a[orb, slab_rows(slab), :] = x_ref[slab, orb]
        pot[slab_rows(slab), :] = x_ref[slab, OWN] + DIAGONAL

    current, previous = field_a, field_b
    steps = schedule()
    for number, (scale, center, back) in enumerate(steps):
        for orb in range(OWN):
            rows = slice(orb * NZ, (orb + 1) * NZ)
            value = current[orb]
            high = value.astype(BF16)
            split[0, rows, :] = high
            split[1, rows, :] = (value - high.astype(F32)).astype(BF16)
        total[...] = (
            jnp.dot(split[0], mh_ref[...], preferred_element_type=F32)
            + jnp.dot(split[0], ml_ref[...], preferred_element_type=F32)
            + jnp.dot(split[1], mh_ref[...], preferred_element_type=F32)
        )
        for orb in range(OWN):
            rows = slice(orb * NZ, (orb + 1) * NZ)
            stack = jnp.concatenate([split[0, rows, :], split[0, rows, :], split[1, rows, :]], axis=0)
            applied = total[rows, :] + jnp.dot(z_ref[...], stack, preferred_element_type=F32)
            following = scale * (applied + (pot[...] - center) * current[orb])
            if number:
                following = following - back * previous[orb]
            previous[orb] = following
            if number == len(steps) - 1:
                put_low(low_ref, orb, following)
                for slab in range(SLABS):
                    out_ref[slab, orb] = following[slab_rows(slab), :]
        current, previous = previous, current


def apply_kernel(x_ref, f_ref, mh_ref, ml_ref, z_ref, app_ref, rest_ref, pot, split, total, rest):
    for slab in range(SLABS):
        for orb in range(OWN):
            rows = slice(orb * NZ + slab * DEPTH, orb * NZ + (slab + 1) * DEPTH)
            total[rows, :] = f_ref[slab, orb]
        pot[slab_rows(slab), :] = x_ref[slab, OWN] + DIAGONAL
    for orb in range(OWN):
        rows = slice(orb * NZ, (orb + 1) * NZ)
        value = total[rows, :]
        high = value.astype(BF16)
        split[0, rows, :] = high
        split[1, rows, :] = (value - high.astype(F32)).astype(BF16)
    total[...] = jnp.dot(split[0], mh_ref[...], preferred_element_type=F32) + jnp.dot(
        split[0], ml_ref[...], preferred_element_type=F32
    )
    rest[...] = jnp.dot(split[1], mh_ref[...], preferred_element_type=F32)
    for orb in range(OWN):
        rows = slice(orb * NZ, (orb + 1) * NZ)
        high, low = split[0, rows, :], split[1, rows, :]
        stack = jnp.concatenate([high, high], axis=0)
        of_low = total[rows, :] + pot[...] * high.astype(F32)
        of_low = of_low + jnp.dot(z_ref[:, : 2 * NZ], stack, preferred_element_type=F32)
        of_rest = rest[rows, :] + pot[...] * low.astype(F32)
        of_rest = of_rest + jnp.dot(z_ref[:, 2 * NZ :], low, preferred_element_type=F32)
        applied_low = (of_low + of_rest).astype(BF16).astype(F32)
        middle = 0.5 * (applied_low + of_low)
        middle_high = middle.astype(BF16).astype(F32)
        put_low(app_ref, orb, middle_high)
        put_low(rest_ref, orb, middle - middle_high)
        put_low(rest_ref, OWN + orb, low.astype(F32))


def run_filter(block):
    plane_high, plane_low, z_stack = (jnp.asarray(matrix) for matrix in stencil_matrices())
    vmem = pl.BlockSpec(memory_space=pltpu.VMEM)
    params = pltpu.CompilerParams(vmem_limit_bytes=KERNEL_BYTES)
    filtered, filtered_low = pl.pallas_call(
        filter_kernel,
        out_shape=(
            jax.ShapeDtypeStruct((SLABS, OWN, DEPTH, PLANE), F32),
            jax.ShapeDtypeStruct((PEERS, OWN, DEPTH, HALF), BF16),
        ),
        in_specs=[vmem] * 4,
        out_specs=(vmem, vmem),
        scratch_shapes=[
            pltpu.VMEM((OWN, NZ, PLANE), F32),
            pltpu.VMEM((OWN, NZ, PLANE), F32),
            pltpu.VMEM((NZ, PLANE), F32),
            pltpu.VMEM((2, OWN * NZ, PLANE), BF16),
            pltpu.VMEM((OWN * NZ, PLANE), F32),
        ],
        compiler_params=params,
        cost_estimate=pl.CostEstimate(flops=5_000_000_000, bytes_accessed=6_000_000, transcendentals=0),
        name="chebyshev",
    )(block, plane_high, plane_low, z_stack)
    applied, rest = pl.pallas_call(
        apply_kernel,
        out_shape=(
            jax.ShapeDtypeStruct((PEERS, OWN, DEPTH, HALF), BF16),
            jax.ShapeDtypeStruct((PEERS, 2 * OWN, DEPTH, HALF), BF16),
        ),
        in_specs=[vmem] * 5,
        out_specs=(vmem, vmem),
        scratch_shapes=[
            pltpu.VMEM((NZ, PLANE), F32),
            pltpu.VMEM((2, OWN * NZ, PLANE), BF16),
            pltpu.VMEM((OWN * NZ, PLANE), F32),
            pltpu.VMEM((OWN * NZ, PLANE), F32),
        ],
        compiler_params=params,
        cost_estimate=pl.CostEstimate(flops=1_000_000_000, bytes_accessed=6_000_000, transcendentals=0),
        name="applied",
    )(block, filtered, plane_high, plane_low, z_stack)
    return filtered_low, applied, rest


def put_pairs(total, shift, keep_ref, send_ref):
    place = lax.rem(lax.axis_index("band"), RING)
    core = lax.rem(lax.axis_index("slab"), 2)
    ring = lax.rem(place + shift + RING, RING)
    mine = lax.rem(ring, 2) == core
    for own in range(2):
        rows = total[own * 192 : (own + 1) * 192]
        gram, cross = rows[:64], rows[64:128] + rows[128:]
        for side in range(2):
            lanes = slice(side * 64, (side + 1) * 64)
            block = jnp.concatenate([gram[:, lanes], cross[:, lanes]], axis=1)
            index = own * RING + side * (RING // 2) + lax.div(ring, 2)
            keep_ref[jnp.where(mine, index, 2 * RING)] = block
            send_ref[jnp.where(mine, 2 * RING, index)] = block


def pair_sum(w_ref, pick):
    total = None
    for depth in range(DEPTH):
        part = lax.dot_general(w_ref[depth], pick(depth), (((1,), (1,)), ((), ())), preferred_element_type=F32)
        total = part if total is None else total + part
    return total


def early_kernel(own_ref, high_ref, rest_ref, *refs):
    blocks, (w_ref, keep_ref, send_ref) = refs[:-3], refs[-3:]
    for side in range(2):
        for place, ref in enumerate((own_ref, high_ref, rest_ref)):
            start = side * 192 + place * 64
            w_ref[:, start : start + 64, :] = ref[:, side * 64 : (side + 1) * 64, :]
    put_pairs(pair_sum(w_ref, lambda depth: own_ref[depth]), 0, keep_ref, send_ref)
    for step in range(1, RING // 2):
        ahead, behind = blocks[2 * step - 2], blocks[2 * step - 1]
        total = pair_sum(w_ref, lambda depth: jnp.concatenate([ahead[depth], behind[depth]], axis=0))
        put_pairs(total[:, :128], -step, keep_ref, send_ref)
        put_pairs(total[:, 128:], step, keep_ref, send_ref)


def late_kernel(w_ref, last_ref, keep_in, send_in, keep_ref, send_ref):
    put_pairs(pair_sum(w_ref, lambda depth: last_ref[depth]), RING // 2, keep_ref, send_ref)


def run_early(own_low, high, rest, blocks):
    vmem = pl.BlockSpec(memory_space=pltpu.VMEM)
    shape = jax.ShapeDtypeStruct((2 * RING + 1, 64, 128), F32)
    return pl.pallas_call(
        early_kernel,
        out_shape=(jax.ShapeDtypeStruct((DEPTH, 6 * 64, HALF), BF16), shape, shape),
        in_specs=[vmem] * (3 + len(blocks)),
        out_specs=(vmem, vmem, vmem),
        compiler_params=pltpu.CompilerParams(vmem_limit_bytes=KERNEL_BYTES),
        cost_estimate=pl.CostEstimate(flops=1_400_000_000, bytes_accessed=6_000_000, transcendentals=0),
        name="pairs_early",
    )(own_low, high, rest, *blocks)


def run_late(weights, last, keep, send):
    vmem = pl.BlockSpec(memory_space=pltpu.VMEM)
    shape = jax.ShapeDtypeStruct(keep.shape, F32)
    return pl.pallas_call(
        late_kernel,
        out_shape=(shape, shape),
        in_specs=[vmem] * 4,
        out_specs=(vmem, vmem),
        input_output_aliases={2: 0, 3: 1},
        compiler_params=pltpu.CompilerParams(vmem_limit_bytes=KERNEL_BYTES),
        cost_estimate=pl.CostEstimate(flops=200_000_000, bytes_accessed=2_000_000, transcendentals=0),
        name="pairs_late",
    )(weights, last, keep, send)


def join_kernel(high_ref, rest_ref, near_ref, far_ref):
    side = lax.div(lax.axis_index("band"), RING)
    for ref, which in ((near_ref, side), (far_ref, 1 - side)):
        sources = pl.ds(which * SLABS, SLABS)
        ref[...] = high_ref[sources].astype(F32) + rest_ref[sources, OWN:].astype(F32)


def run_join(high, rest):
    vmem = pl.BlockSpec(memory_space=pltpu.VMEM)
    shape = jax.ShapeDtypeStruct((SLABS, OWN, DEPTH, HALF), F32)
    return pl.pallas_call(
        join_kernel,
        out_shape=(shape, shape),
        in_specs=[vmem, vmem],
        out_specs=(vmem, vmem),
        compiler_params=pltpu.CompilerParams(vmem_limit_bytes=KERNEL_BYTES),
        cost_estimate=pl.CostEstimate(flops=1_000_000, bytes_accessed=2_000_000, transcendentals=0),
        name="join",
    )(high, rest)


def place_kernel(near_ref, far_ref, out_ref, done):
    side = lax.div(lax.axis_index("band"), RING)
    copies = []
    for number, (ref, which) in enumerate(((near_ref, side), (far_ref, 1 - side))):
        lanes = pl.ds(pl.multiple_of(which * HALF, HALF), HALF)
        copies.append(pltpu.make_async_copy(ref, out_ref.at[:, :, :, lanes], done.at[number]))
    for copy in copies:
        copy.start()
    for copy in copies:
        copy.wait()


def run_place(near, far):
    vmem = pl.BlockSpec(memory_space=pltpu.VMEM)
    return pl.pallas_call(
        place_kernel,
        out_shape=jax.ShapeDtypeStruct((SLABS, OWN, DEPTH, PLANE), F32),
        in_specs=[vmem, vmem],
        out_specs=pl.BlockSpec(memory_space=pl.ANY),
        scratch_shapes=[pltpu.SemaphoreType.DMA((2,))],
        compiler_params=pltpu.CompilerParams(vmem_limit_bytes=KERNEL_BYTES),
        cost_estimate=pl.CostEstimate(flops=0, bytes_accessed=2_000_000, transcendentals=0),
        name="place",
    )(near, far)


def plane_groups():
    return [[(side * RING + ring) * SLABS + slab for side in range(2) for slab in range(SLABS)] for ring in range(RING)]


def core_groups():
    return [
        [(side * RING + ring) * SLABS + 2 * chip + core for side in range(2) for chip in range(SLABS // 2)]
        for ring in range(RING)
        for core in range(2)
    ]


def ring_pairs(even, odd):
    pairs = []
    for side in range(2):
        for ring in range(RING):
            for slab in range(SLABS):
                step = odd if slab % 2 else even
                pairs.append(((side * RING + ring) * SLABS + slab, (side * RING + (ring + step) % RING) * SLABS + slab))
    return pairs


def side_pairs():
    return [(place, place ^ (RING * SLABS)) for place in range(2 * RING * SLABS)]


def core_pairs():
    return [(place, place ^ 1) for place in range(2 * RING * SLABS)]


def over_plane(block):
    return lax.all_to_all(block, BOTH, 0, 0, axis_index_groups=plane_groups(), tiled=True)


def by_depth(block):
    return block.reshape(PEERS * OWN, DEPTH, HALF).transpose(1, 0, 2)


def after(value, *earlier):
    return lax.optimization_barrier((value, *earlier))[0]


def on_device(orbitals, potential):
    block = orbitals.reshape(SLABS, OWN, DEPTH, PLANE)
    shared = jnp.broadcast_to(potential[None, None], (SLABS, 1, DEPTH, PLANE))
    block = lax.all_to_all(jnp.concatenate([block, shared], axis=1), "slab", 0, 0, tiled=True)
    filtered_low, applied, rest = run_filter(block)
    filtered_low = over_plane(filtered_low)
    own_low = by_depth(filtered_low)
    ahead = lax.ppermute(own_low, BOTH, ring_pairs(1, 1))
    behind = lax.ppermute(own_low, BOTH, ring_pairs(-1, -1))
    blocks = [ahead, behind]
    high = over_plane(applied)
    ahead, behind, applied = lax.optimization_barrier((ahead, behind, applied))
    ahead = lax.ppermute(ahead, BOTH, ring_pairs(1, 1))
    behind = lax.ppermute(behind, BOTH, ring_pairs(-1, -1))
    blocks += [ahead, behind]
    ahead, behind, high = lax.optimization_barrier((ahead, behind, high))
    rest = over_plane(rest)
    ahead = lax.ppermute(ahead, BOTH, ring_pairs(1, 1))
    behind = lax.ppermute(behind, BOTH, ring_pairs(-1, -1))
    blocks += [ahead, behind]
    ahead, behind, rest = lax.optimization_barrier((ahead, behind, rest))
    last = jnp.where(lax.axis_index("slab") % 2 == 0, ahead, behind)
    last = lax.ppermute(last, BOTH, ring_pairs(1, -1))
    weights, keep, send = run_early(own_low, by_depth(high), by_depth(rest[:, :OWN]), blocks)
    near, far = run_join(filtered_low, rest)
    far = lax.ppermute(far, BOTH, side_pairs())
    filtered = run_place(near, far)
    last, filtered = lax.optimization_barrier((last, filtered))
    keep, send = run_late(weights, last, keep, send)
    sums = (keep + lax.ppermute(send, BOTH, core_pairs()))[: 2 * RING]
    sums = lax.all_to_all(sums, BOTH, 0, 0, axis_index_groups=core_groups(), tiled=True)
    sums = jnp.sum(sums, axis=0) / NCELLS
    return filtered.reshape(SLABS * OWN, DEPTH, PLANE), sums[:, :64], sums[:, 64:]


def solution(mesh):
    return jax.shard_map(
        on_device,
        mesh=mesh,
        in_specs=(P("band", "slab", None), P("slab", None)),
        out_specs=(P("band", "slab", None), P("band", "slab"), P("band", "slab")),
        check_vma=False,
    )
```

```python
import jax
import jax.numpy as jnp
import numpy as np
from jax import lax
from jax.experimental import pallas as pl
from jax.experimental.pallas import tpu as pltpu
from jax.sharding import PartitionSpec as P

DEGREE = 4
NY = 16
NX = 32
NZ = 128
PLANE = NX * NY
NCELLS = NZ * PLANE
SLABS = 16
DEPTH = NZ // SLABS
OWN = 4
HALF = PLANE // 2
RING = 8
PEERS = 32

COEFFS = (
    -5369.0 / 1800.0,
    12.0 / 7.0,
    -15.0 / 56.0,
    10.0 / 189.0,
    -1.0 / 112.0,
    2.0 / 1925.0,
    -1.0 / 16632.0,
)
SPACING = 0.6
LOWER = -2.0
CUTOFF = 8.0
UPPER = 32.0
KINETIC = -0.5 / SPACING**2
DIAGONAL = 3.0 * COEFFS[0] * KINETIC
BF16 = jnp.bfloat16
F32 = jnp.float32
BOTH = ("band", "slab")
KERNEL_BYTES = 16 * 1024 * 1024


def line_matrix(size):
    matrix = np.zeros((size, size))
    for reach in range(1, 7):
        matrix += KINETIC * COEFFS[reach] * (np.eye(size, k=reach) + np.eye(size, k=-reach))
    return matrix


def two_terms(matrix):
    high = matrix.astype(jnp.bfloat16)
    low = (matrix - high.astype(np.float64)).astype(jnp.bfloat16)
    return high, low


def stencil_matrices():
    plane = np.kron(line_matrix(NX), np.eye(NY)) + np.kron(np.eye(NX), line_matrix(NY))
    plane_high, plane_low = two_terms(plane)
    z_high, z_low = two_terms(line_matrix(NZ))
    return plane_high, plane_low, np.concatenate([z_high, z_low, z_high], axis=1)


def schedule():
    half_width = (UPPER - CUTOFF) / 2.0
    center = (UPPER + CUTOFF) / 2.0
    sigma_first = half_width / (LOWER - center)
    sigma = sigma_first
    steps = [(sigma_first / half_width, center, 0.0)]
    for _ in range(DEGREE - 1):
        sigma_next = 1.0 / (2.0 / sigma_first - sigma)
        steps.append((2.0 * sigma_next / half_width, center, sigma * sigma_next))
        sigma = sigma_next
    return steps


def slab_rows(slab):
    return slice(slab * DEPTH, (slab + 1) * DEPTH)


def put_low(ref, orb, value):
    for slab in range(SLABS):
        for side in range(2):
            ref[side * SLABS + slab, orb] = value[slab_rows(slab), side * HALF : (side + 1) * HALF].astype(BF16)


def filter_kernel(x_ref, mh_ref, ml_ref, z_ref, out_ref, low_ref, rest_ref, field_a, field_b, pot, split, total):
    for slab in range(SLABS):
        for orb in range(OWN):
            field_a[orb, slab_rows(slab), :] = x_ref[slab, orb]
        pot[slab_rows(slab), :] = x_ref[slab, OWN] + DIAGONAL

    current, previous = field_a, field_b
    steps = schedule()
    for number, (scale, center, back) in enumerate(steps):
        for orb in range(OWN):
            rows = slice(orb * NZ, (orb + 1) * NZ)
            value = current[orb]
            high = value.astype(BF16)
            split[0, rows, :] = high
            split[1, rows, :] = (value - high.astype(F32)).astype(BF16)
        total[...] = (
            jnp.dot(split[0], mh_ref[...], preferred_element_type=F32)
            + jnp.dot(split[0], ml_ref[...], preferred_element_type=F32)
            + jnp.dot(split[1], mh_ref[...], preferred_element_type=F32)
        )
        for orb in range(OWN):
            rows = slice(orb * NZ, (orb + 1) * NZ)
            stack = jnp.concatenate([split[0, rows, :], split[0, rows, :], split[1, rows, :]], axis=0)
            applied = total[rows, :] + jnp.dot(z_ref[...], stack, preferred_element_type=F32)
            following = scale * (applied + (pot[...] - center) * current[orb])
            if number:
                following = following - back * previous[orb]
            previous[orb] = following
            if number == len(steps) - 1:
                high = following.astype(BF16).astype(F32)
                put_low(low_ref, orb, high)
                put_low(rest_ref, orb, following - high)
                for slab in range(SLABS):
                    out_ref[slab, orb] = following[slab_rows(slab), :]
        current, previous = previous, current


def apply_kernel(x_ref, f_ref, mh_ref, ml_ref, z_ref, app_ref, pot, split, total, rest):
    for slab in range(SLABS):
        for orb in range(OWN):
            rows = slice(orb * NZ + slab * DEPTH, orb * NZ + (slab + 1) * DEPTH)
            total[rows, :] = f_ref[slab, orb]
        pot[slab_rows(slab), :] = x_ref[slab, OWN] + DIAGONAL
    for orb in range(OWN):
        rows = slice(orb * NZ, (orb + 1) * NZ)
        value = total[rows, :]
        high = value.astype(BF16)
        split[0, rows, :] = high
        split[1, rows, :] = (value - high.astype(F32)).astype(BF16)
    total[...] = jnp.dot(split[0], mh_ref[...], preferred_element_type=F32) + jnp.dot(
        split[0], ml_ref[...], preferred_element_type=F32
    )
    rest[...] = jnp.dot(split[1], mh_ref[...], preferred_element_type=F32)
    for orb in range(OWN):
        rows = slice(orb * NZ, (orb + 1) * NZ)
        high, low = split[0, rows, :], split[1, rows, :]
        stack = jnp.concatenate([high, high], axis=0)
        of_low = total[rows, :] + pot[...] * high.astype(F32)
        of_low = of_low + jnp.dot(z_ref[:, : 2 * NZ], stack, preferred_element_type=F32)
        of_rest = rest[rows, :] + pot[...] * low.astype(F32)
        of_rest = of_rest + jnp.dot(z_ref[:, 2 * NZ :], low, preferred_element_type=F32)
        applied_low = (of_low + of_rest).astype(BF16).astype(F32)
        middle = 0.5 * (applied_low + of_low)
        middle_high = middle.astype(BF16).astype(F32)
        put_low(app_ref, orb, middle_high)
        put_low(app_ref, OWN + orb, middle - middle_high)


def run_filter(block):
    plane_high, plane_low, z_stack = (jnp.asarray(matrix) for matrix in stencil_matrices())
    vmem = pl.BlockSpec(memory_space=pltpu.VMEM)
    params = pltpu.CompilerParams(vmem_limit_bytes=KERNEL_BYTES)
    filtered, filtered_low, filtered_rest = pl.pallas_call(
        filter_kernel,
        out_shape=(
            jax.ShapeDtypeStruct((SLABS, OWN, DEPTH, PLANE), F32),
            jax.ShapeDtypeStruct((PEERS, OWN, DEPTH, HALF), BF16),
            jax.ShapeDtypeStruct((PEERS, OWN, DEPTH, HALF), BF16),
        ),
        in_specs=[vmem] * 4,
        out_specs=(vmem, vmem, vmem),
        scratch_shapes=[
            pltpu.VMEM((OWN, NZ, PLANE), F32),
            pltpu.VMEM((OWN, NZ, PLANE), F32),
            pltpu.VMEM((NZ, PLANE), F32),
            pltpu.VMEM((2, OWN * NZ, PLANE), BF16),
            pltpu.VMEM((OWN * NZ, PLANE), F32),
        ],
        compiler_params=params,
        cost_estimate=pl.CostEstimate(flops=5_000_000_000, bytes_accessed=6_000_000, transcendentals=0),
        name="chebyshev",
    )(block, plane_high, plane_low, z_stack)
    applied = pl.pallas_call(
        apply_kernel,
        out_shape=jax.ShapeDtypeStruct((PEERS, 2 * OWN, DEPTH, HALF), BF16),
        in_specs=[vmem] * 5,
        out_specs=vmem,
        scratch_shapes=[
            pltpu.VMEM((NZ, PLANE), F32),
            pltpu.VMEM((2, OWN * NZ, PLANE), BF16),
            pltpu.VMEM((OWN * NZ, PLANE), F32),
            pltpu.VMEM((OWN * NZ, PLANE), F32),
        ],
        compiler_params=params,
        cost_estimate=pl.CostEstimate(flops=1_000_000_000, bytes_accessed=6_000_000, transcendentals=0),
        name="applied",
    )(block, filtered, plane_high, plane_low, z_stack)
    return filtered_low, filtered_rest, applied


def put_pairs(total, shift, keep_ref, send_ref):
    place = lax.rem(lax.axis_index("band"), RING)
    core = lax.rem(lax.axis_index("slab"), 2)
    ring = lax.rem(place + shift + RING, RING)
    mine = lax.rem(ring, 2) == core
    for own in range(2):
        rows = total[own * 192 : (own + 1) * 192]
        gram, cross = rows[:64], rows[64:128] + rows[128:]
        for side in range(2):
            lanes = slice(side * 64, (side + 1) * 64)
            block = jnp.concatenate([gram[:, lanes], cross[:, lanes]], axis=1)
            index = own * RING + side * (RING // 2) + lax.div(ring, 2)
            keep_ref[jnp.where(mine, index, 2 * RING)] = block
            send_ref[jnp.where(mine, 2 * RING, index)] = block


def pair_sum(w_ref, pick):
    total = None
    for depth in range(DEPTH):
        part = lax.dot_general(w_ref[depth], pick(depth), (((1,), (1,)), ((), ())), preferred_element_type=F32)
        total = part if total is None else total + part
    return total


def early_kernel(own_ref, high_ref, rest_ref, *refs):
    blocks, (w_ref, keep_ref, send_ref) = refs[:-3], refs[-3:]
    for side in range(2):
        for place, ref in enumerate((own_ref, high_ref, rest_ref)):
            start = side * 192 + place * 64
            w_ref[:, start : start + 64, :] = ref[:, side * 64 : (side + 1) * 64, :]
    put_pairs(pair_sum(w_ref, lambda depth: own_ref[depth]), 0, keep_ref, send_ref)
    for step in range(1, RING // 2):
        ahead, behind = blocks[2 * step - 2], blocks[2 * step - 1]
        total = pair_sum(w_ref, lambda depth: jnp.concatenate([ahead[depth], behind[depth]], axis=0))
        put_pairs(total[:, :128], -step, keep_ref, send_ref)
        put_pairs(total[:, 128:], step, keep_ref, send_ref)


def late_kernel(w_ref, last_ref, keep_in, send_in, keep_ref, send_ref):
    put_pairs(pair_sum(w_ref, lambda depth: last_ref[depth]), RING // 2, keep_ref, send_ref)


def run_early(own_low, high, rest, blocks):
    vmem = pl.BlockSpec(memory_space=pltpu.VMEM)
    shape = jax.ShapeDtypeStruct((2 * RING + 1, 64, 128), F32)
    return pl.pallas_call(
        early_kernel,
        out_shape=(jax.ShapeDtypeStruct((DEPTH, 6 * 64, HALF), BF16), shape, shape),
        in_specs=[vmem] * (3 + len(blocks)),
        out_specs=(vmem, vmem, vmem),
        compiler_params=pltpu.CompilerParams(vmem_limit_bytes=KERNEL_BYTES),
        cost_estimate=pl.CostEstimate(flops=1_400_000_000, bytes_accessed=6_000_000, transcendentals=0),
        name="pairs_early",
    )(own_low, high, rest, *blocks)


def run_late(weights, last, keep, send):
    vmem = pl.BlockSpec(memory_space=pltpu.VMEM)
    shape = jax.ShapeDtypeStruct(keep.shape, F32)
    return pl.pallas_call(
        late_kernel,
        out_shape=(shape, shape),
        in_specs=[vmem] * 4,
        out_specs=(vmem, vmem),
        input_output_aliases={2: 0, 3: 1},
        compiler_params=pltpu.CompilerParams(vmem_limit_bytes=KERNEL_BYTES),
        cost_estimate=pl.CostEstimate(flops=200_000_000, bytes_accessed=2_000_000, transcendentals=0),
        name="pairs_late",
    )(weights, last, keep, send)


def join_kernel(high_ref, rest_ref, near_ref, far_ref):
    side = lax.div(lax.axis_index("band"), RING)
    for ref, which in ((near_ref, side), (far_ref, 1 - side)):
        sources = pl.ds(which * SLABS, SLABS)
        ref[...] = high_ref[sources].astype(F32) + rest_ref[sources].astype(F32)


def run_join(high, rest):
    vmem = pl.BlockSpec(memory_space=pltpu.VMEM)
    shape = jax.ShapeDtypeStruct((SLABS, OWN, DEPTH, HALF), F32)
    return pl.pallas_call(
        join_kernel,
        out_shape=(shape, shape),
        in_specs=[vmem, vmem],
        out_specs=(vmem, vmem),
        compiler_params=pltpu.CompilerParams(vmem_limit_bytes=KERNEL_BYTES),
        cost_estimate=pl.CostEstimate(flops=1_000_000, bytes_accessed=2_000_000, transcendentals=0),
        name="join",
    )(high, rest)


def place_kernel(near_ref, far_ref, out_ref, done):
    side = lax.div(lax.axis_index("band"), RING)
    copies = []
    for number, (ref, which) in enumerate(((near_ref, side), (far_ref, 1 - side))):
        lanes = pl.ds(pl.multiple_of(which * HALF, HALF), HALF)
        copies.append(pltpu.make_async_copy(ref, out_ref.at[:, :, :, lanes], done.at[number]))
    for copy in copies:
        copy.start()
    for copy in copies:
        copy.wait()


def run_place(near, far):
    vmem = pl.BlockSpec(memory_space=pltpu.VMEM)
    return pl.pallas_call(
        place_kernel,
        out_shape=jax.ShapeDtypeStruct((SLABS, OWN, DEPTH, PLANE), F32),
        in_specs=[vmem, vmem],
        out_specs=pl.BlockSpec(memory_space=pl.ANY),
        scratch_shapes=[pltpu.SemaphoreType.DMA((2,))],
        compiler_params=pltpu.CompilerParams(vmem_limit_bytes=KERNEL_BYTES),
        cost_estimate=pl.CostEstimate(flops=0, bytes_accessed=2_000_000, transcendentals=0),
        name="place",
    )(near, far)


def plane_groups():
    return [[(side * RING + ring) * SLABS + slab for side in range(2) for slab in range(SLABS)] for ring in range(RING)]


def core_groups():
    return [
        [(side * RING + ring) * SLABS + 2 * chip + core for side in range(2) for chip in range(SLABS // 2)]
        for ring in range(RING)
        for core in range(2)
    ]


def ring_pairs(even, odd):
    pairs = []
    for side in range(2):
        for ring in range(RING):
            for slab in range(SLABS):
                step = odd if slab % 2 else even
                pairs.append(((side * RING + ring) * SLABS + slab, (side * RING + (ring + step) % RING) * SLABS + slab))
    return pairs


def side_pairs():
    return [(place, place ^ (RING * SLABS)) for place in range(2 * RING * SLABS)]


def core_pairs():
    return [(place, place ^ 1) for place in range(2 * RING * SLABS)]


def over_plane(block):
    return lax.all_to_all(block, BOTH, 0, 0, axis_index_groups=plane_groups(), tiled=True)


def by_depth(block):
    return block.reshape(PEERS * OWN, DEPTH, HALF).transpose(1, 0, 2)


def after(value, *earlier):
    return lax.optimization_barrier((value, *earlier))[0]


def on_device(orbitals, potential):
    block = orbitals.reshape(SLABS, OWN, DEPTH, PLANE)
    shared = jnp.broadcast_to(potential[None, None], (SLABS, 1, DEPTH, PLANE))
    block = lax.all_to_all(jnp.concatenate([block, shared], axis=1), "slab", 0, 0, tiled=True)
    filtered_low, filtered_rest, applied = run_filter(block)
    filtered_low = over_plane(filtered_low)
    own_low = by_depth(filtered_low)
    ahead = lax.ppermute(own_low, BOTH, ring_pairs(1, 1))
    behind = lax.ppermute(own_low, BOTH, ring_pairs(-1, -1))
    blocks = [ahead, behind]
    filtered_rest = over_plane(filtered_rest)
    ahead, applied = lax.optimization_barrier((ahead, applied))
    behind, applied = lax.optimization_barrier((behind, applied))
    ahead = lax.ppermute(ahead, BOTH, ring_pairs(1, 1))
    behind = lax.ppermute(behind, BOTH, ring_pairs(-1, -1))
    blocks += [ahead, behind]
    ahead, filtered_rest = lax.optimization_barrier((ahead, filtered_rest))
    behind, filtered_rest = lax.optimization_barrier((behind, filtered_rest))
    applied = over_plane(applied)
    ahead = lax.ppermute(ahead, BOTH, ring_pairs(1, 1))
    behind = lax.ppermute(behind, BOTH, ring_pairs(-1, -1))
    blocks += [ahead, behind]
    ahead, applied = lax.optimization_barrier((ahead, applied))
    behind, applied = lax.optimization_barrier((behind, applied))
    last = jnp.where(lax.axis_index("slab") % 2 == 0, ahead, behind)
    last = lax.ppermute(last, BOTH, ring_pairs(1, -1))
    weights, keep, send = run_early(own_low, by_depth(applied[:, :OWN]), by_depth(applied[:, OWN:]), blocks)
    near, far = run_join(filtered_low, filtered_rest)
    far = lax.ppermute(far, BOTH, side_pairs())
    filtered = run_place(near, after(far, keep))
    last, filtered = lax.optimization_barrier((last, filtered))
    keep, send = run_late(weights, last, keep, send)
    sums = (keep + lax.ppermute(send, BOTH, core_pairs()))[: 2 * RING]
    sums = lax.all_to_all(sums, BOTH, 0, 0, axis_index_groups=core_groups(), tiled=True)
    sums = jnp.sum(sums, axis=0) / NCELLS
    return filtered.reshape(SLABS * OWN, DEPTH, PLANE), sums[:, :64], sums[:, 64:]


def solution(mesh):
    return jax.shard_map(
        on_device,
        mesh=mesh,
        in_specs=(P("band", "slab", None), P("slab", None)),
        out_specs=(P("band", "slab", None), P("band", "slab"), P("band", "slab")),
        check_vma=False,
    )
```

```python
import jax
import jax.numpy as jnp
import numpy as np
from jax import lax
from jax.experimental import pallas as pl
from jax.experimental.pallas import tpu as pltpu
from jax.sharding import PartitionSpec as P

DEGREE = 4
NY = 16
NX = 32
NZ = 128
PLANE = NX * NY
NCELLS = NZ * PLANE
SLABS = 16
DEPTH = NZ // SLABS
OWN = 4
HALF = PLANE // 2
RING = 8
PEERS = 32

COEFFS = (
    -5369.0 / 1800.0,
    12.0 / 7.0,
    -15.0 / 56.0,
    10.0 / 189.0,
    -1.0 / 112.0,
    2.0 / 1925.0,
    -1.0 / 16632.0,
)
SPACING = 0.6
LOWER = -2.0
CUTOFF = 8.0
UPPER = 32.0
KINETIC = -0.5 / SPACING**2
DIAGONAL = 3.0 * COEFFS[0] * KINETIC
BF16 = jnp.bfloat16
F32 = jnp.float32
BOTH = ("band", "slab")
KERNEL_BYTES = 16 * 1024 * 1024


def line_matrix(size):
    matrix = np.zeros((size, size))
    for reach in range(1, 7):
        matrix += KINETIC * COEFFS[reach] * (np.eye(size, k=reach) + np.eye(size, k=-reach))
    return matrix


def two_terms(matrix):
    high = matrix.astype(jnp.bfloat16)
    low = (matrix - high.astype(np.float64)).astype(jnp.bfloat16)
    return high, low


def stencil_matrices():
    plane = np.kron(line_matrix(NX), np.eye(NY)) + np.kron(np.eye(NX), line_matrix(NY))
    plane_high, plane_low = two_terms(plane)
    z_high, z_low = two_terms(line_matrix(NZ))
    return plane_high, plane_low, np.concatenate([z_high, z_low, z_high], axis=1)


def schedule():
    half_width = (UPPER - CUTOFF) / 2.0
    center = (UPPER + CUTOFF) / 2.0
    sigma_first = half_width / (LOWER - center)
    sigma = sigma_first
    steps = [(sigma_first / half_width, center, 0.0)]
    for _ in range(DEGREE - 1):
        sigma_next = 1.0 / (2.0 / sigma_first - sigma)
        steps.append((2.0 * sigma_next / half_width, center, sigma * sigma_next))
        sigma = sigma_next
    return steps


def slab_rows(slab):
    return slice(slab * DEPTH, (slab + 1) * DEPTH)


def put_low(ref, orb, value):
    for slab in range(SLABS):
        for side in range(2):
            ref[side * SLABS + slab, orb] = value[slab_rows(slab), side * HALF : (side + 1) * HALF].astype(BF16)


def filter_kernel(x_ref, mh_ref, ml_ref, z_ref, out_ref, low_ref, rest_ref, field_a, field_b, pot, split, total):
    for slab in range(SLABS):
        for orb in range(OWN):
            field_a[orb, slab_rows(slab), :] = x_ref[slab, orb]
        pot[slab_rows(slab), :] = x_ref[slab, OWN] + DIAGONAL

    current, previous = field_a, field_b
    steps = schedule()
    for number, (scale, center, back) in enumerate(steps):
        for orb in range(OWN):
            rows = slice(orb * NZ, (orb + 1) * NZ)
            value = current[orb]
            high = value.astype(BF16)
            split[0, rows, :] = high
            split[1, rows, :] = (value - high.astype(F32)).astype(BF16)
        total[...] = (
            jnp.dot(split[0], mh_ref[...], preferred_element_type=F32)
            + jnp.dot(split[0], ml_ref[...], preferred_element_type=F32)
            + jnp.dot(split[1], mh_ref[...], preferred_element_type=F32)
        )
        for orb in range(OWN):
            rows = slice(orb * NZ, (orb + 1) * NZ)
            stack = jnp.concatenate([split[0, rows, :], split[0, rows, :], split[1, rows, :]], axis=0)
            applied = total[rows, :] + jnp.dot(z_ref[...], stack, preferred_element_type=F32)
            following = scale * (applied + (pot[...] - center) * current[orb])
            if number:
                following = following - back * previous[orb]
            previous[orb] = following
            if number == len(steps) - 1:
                high = following.astype(BF16).astype(F32)
                put_low(low_ref, orb, high)
                put_low(rest_ref, orb, following - high)
                for slab in range(SLABS):
                    out_ref[slab, orb] = following[slab_rows(slab), :]
        current, previous = previous, current


def apply_kernel(x_ref, f_ref, mh_ref, ml_ref, z_ref, app_ref, pot, split, total, rest):
    for slab in range(SLABS):
        for orb in range(OWN):
            rows = slice(orb * NZ + slab * DEPTH, orb * NZ + (slab + 1) * DEPTH)
            total[rows, :] = f_ref[slab, orb]
        pot[slab_rows(slab), :] = x_ref[slab, OWN] + DIAGONAL
    for orb in range(OWN):
        rows = slice(orb * NZ, (orb + 1) * NZ)
        value = total[rows, :]
        high = value.astype(BF16)
        split[0, rows, :] = high
        split[1, rows, :] = (value - high.astype(F32)).astype(BF16)
    total[...] = jnp.dot(split[0], mh_ref[...], preferred_element_type=F32) + jnp.dot(
        split[0], ml_ref[...], preferred_element_type=F32
    )
    rest[...] = jnp.dot(split[1], mh_ref[...], preferred_element_type=F32)
    for orb in range(OWN):
        rows = slice(orb * NZ, (orb + 1) * NZ)
        high, low = split[0, rows, :], split[1, rows, :]
        stack = jnp.concatenate([high, high], axis=0)
        of_low = total[rows, :] + pot[...] * high.astype(F32)
        of_low = of_low + jnp.dot(z_ref[:, : 2 * NZ], stack, preferred_element_type=F32)
        of_rest = rest[rows, :] + pot[...] * low.astype(F32)
        of_rest = of_rest + jnp.dot(z_ref[:, 2 * NZ :], low, preferred_element_type=F32)
        applied_low = (of_low + of_rest).astype(BF16).astype(F32)
        middle = 0.5 * (applied_low + of_low)
        middle_high = middle.astype(BF16).astype(F32)
        put_low(app_ref, orb, middle_high)
        put_low(app_ref, OWN + orb, middle - middle_high)


def run_filter(block):
    plane_high, plane_low, z_stack = (jnp.asarray(matrix) for matrix in stencil_matrices())
    vmem = pl.BlockSpec(memory_space=pltpu.VMEM)
    params = pltpu.CompilerParams(vmem_limit_bytes=KERNEL_BYTES)
    filtered, filtered_low, filtered_rest = pl.pallas_call(
        filter_kernel,
        out_shape=(
            jax.ShapeDtypeStruct((SLABS, OWN, DEPTH, PLANE), F32),
            jax.ShapeDtypeStruct((PEERS, OWN, DEPTH, HALF), BF16),
            jax.ShapeDtypeStruct((PEERS, OWN, DEPTH, HALF), BF16),
        ),
        in_specs=[vmem] * 4,
        out_specs=(vmem, vmem, vmem),
        scratch_shapes=[
            pltpu.VMEM((OWN, NZ, PLANE), F32),
            pltpu.VMEM((OWN, NZ, PLANE), F32),
            pltpu.VMEM((NZ, PLANE), F32),
            pltpu.VMEM((2, OWN * NZ, PLANE), BF16),
            pltpu.VMEM((OWN * NZ, PLANE), F32),
        ],
        compiler_params=params,
        cost_estimate=pl.CostEstimate(flops=5_000_000_000, bytes_accessed=6_000_000, transcendentals=0),
        name="chebyshev",
    )(block, plane_high, plane_low, z_stack)
    applied = pl.pallas_call(
        apply_kernel,
        out_shape=jax.ShapeDtypeStruct((PEERS, 2 * OWN, DEPTH, HALF), BF16),
        in_specs=[vmem] * 5,
        out_specs=vmem,
        scratch_shapes=[
            pltpu.VMEM((NZ, PLANE), F32),
            pltpu.VMEM((2, OWN * NZ, PLANE), BF16),
            pltpu.VMEM((OWN * NZ, PLANE), F32),
            pltpu.VMEM((OWN * NZ, PLANE), F32),
        ],
        compiler_params=params,
        cost_estimate=pl.CostEstimate(flops=1_000_000_000, bytes_accessed=6_000_000, transcendentals=0),
        name="applied",
    )(block, filtered, plane_high, plane_low, z_stack)
    return filtered_low, filtered_rest, applied


def put_pairs(total, shift, keep_ref, send_ref):
    place = lax.rem(lax.axis_index("band"), RING)
    core = lax.rem(lax.axis_index("slab"), 2)
    ring = lax.rem(place + shift + RING, RING)
    mine = lax.rem(ring, 2) == core
    for own in range(2):
        rows = total[own * 192 : (own + 1) * 192]
        gram, cross = rows[:64], rows[64:128] + rows[128:]
        for side in range(2):
            lanes = slice(side * 64, (side + 1) * 64)
            block = jnp.concatenate([gram[:, lanes], cross[:, lanes]], axis=1)
            index = own * RING + side * (RING // 2) + lax.div(ring, 2)
            keep_ref[jnp.where(mine, index, 2 * RING)] = block
            send_ref[jnp.where(mine, 2 * RING, index)] = block


def pair_sum(w_ref, pick):
    total = None
    for depth in range(DEPTH):
        part = lax.dot_general(w_ref[depth], pick(depth), (((1,), (1,)), ((), ())), preferred_element_type=F32)
        total = part if total is None else total + part
    return total


def early_kernel(own_ref, high_ref, rest_ref, *refs):
    blocks, (w_ref, keep_ref, send_ref) = refs[:-3], refs[-3:]
    for side in range(2):
        for place, ref in enumerate((own_ref, high_ref, rest_ref)):
            start = side * 192 + place * 64
            w_ref[:, start : start + 64, :] = ref[:, side * 64 : (side + 1) * 64, :]
    put_pairs(pair_sum(w_ref, lambda depth: own_ref[depth]), 0, keep_ref, send_ref)
    for step in range(1, RING // 2):
        ahead, behind = blocks[2 * step - 2], blocks[2 * step - 1]
        total = pair_sum(w_ref, lambda depth: jnp.concatenate([ahead[depth], behind[depth]], axis=0))
        put_pairs(total[:, :128], -step, keep_ref, send_ref)
        put_pairs(total[:, 128:], step, keep_ref, send_ref)


def late_kernel(w_ref, last_ref, keep_in, send_in, keep_ref, send_ref):
    put_pairs(pair_sum(w_ref, lambda depth: last_ref[depth]), RING // 2, keep_ref, send_ref)


def run_early(own_low, high, rest, blocks):
    vmem = pl.BlockSpec(memory_space=pltpu.VMEM)
    shape = jax.ShapeDtypeStruct((2 * RING + 1, 64, 128), F32)
    return pl.pallas_call(
        early_kernel,
        out_shape=(jax.ShapeDtypeStruct((DEPTH, 6 * 64, HALF), BF16), shape, shape),
        in_specs=[vmem] * (3 + len(blocks)),
        out_specs=(vmem, vmem, vmem),
        compiler_params=pltpu.CompilerParams(vmem_limit_bytes=KERNEL_BYTES),
        cost_estimate=pl.CostEstimate(flops=1_400_000_000, bytes_accessed=6_000_000, transcendentals=0),
        name="pairs_early",
    )(own_low, high, rest, *blocks)


def run_late(weights, last, keep, send):
    vmem = pl.BlockSpec(memory_space=pltpu.VMEM)
    shape = jax.ShapeDtypeStruct(keep.shape, F32)
    return pl.pallas_call(
        late_kernel,
        out_shape=(shape, shape),
        in_specs=[vmem] * 4,
        out_specs=(vmem, vmem),
        input_output_aliases={2: 0, 3: 1},
        compiler_params=pltpu.CompilerParams(vmem_limit_bytes=KERNEL_BYTES),
        cost_estimate=pl.CostEstimate(flops=200_000_000, bytes_accessed=2_000_000, transcendentals=0),
        name="pairs_late",
    )(weights, last, keep, send)


def join_kernel(own_ref, rest_ref, near_ref, far_ref):
    side = lax.div(lax.axis_index("band"), RING)
    for ref, which in ((near_ref, side), (far_ref, 1 - side)):
        rows = pl.ds(pl.multiple_of(which * 64, 64), 64)
        high = jnp.swapaxes(own_ref[:, rows, :].astype(F32), 0, 1).reshape(SLABS, OWN, DEPTH, HALF)
        ref[...] = high + rest_ref[pl.ds(which * SLABS, SLABS)].astype(F32)


def run_join(own_low, rest):
    vmem = pl.BlockSpec(memory_space=pltpu.VMEM)
    shape = jax.ShapeDtypeStruct((SLABS, OWN, DEPTH, HALF), F32)
    return pl.pallas_call(
        join_kernel,
        out_shape=(shape, shape),
        in_specs=[vmem, vmem],
        out_specs=(vmem, vmem),
        compiler_params=pltpu.CompilerParams(vmem_limit_bytes=KERNEL_BYTES),
        cost_estimate=pl.CostEstimate(flops=1_000_000, bytes_accessed=2_000_000, transcendentals=0),
        name="join",
    )(own_low, rest)


def place_kernel(near_ref, far_ref, out_ref, done):
    side = lax.div(lax.axis_index("band"), RING)
    copies = []
    for number, (ref, which) in enumerate(((near_ref, side), (far_ref, 1 - side))):
        lanes = pl.ds(pl.multiple_of(which * HALF, HALF), HALF)
        copies.append(pltpu.make_async_copy(ref, out_ref.at[:, :, :, lanes], done.at[number]))
    for copy in copies:
        copy.start()
    for copy in copies:
        copy.wait()


def run_place(near, far):
    vmem = pl.BlockSpec(memory_space=pltpu.VMEM)
    return pl.pallas_call(
        place_kernel,
        out_shape=jax.ShapeDtypeStruct((SLABS, OWN, DEPTH, PLANE), F32),
        in_specs=[vmem, vmem],
        out_specs=pl.BlockSpec(memory_space=pl.ANY),
        scratch_shapes=[pltpu.SemaphoreType.DMA((2,))],
        compiler_params=pltpu.CompilerParams(vmem_limit_bytes=KERNEL_BYTES),
        cost_estimate=pl.CostEstimate(flops=0, bytes_accessed=2_000_000, transcendentals=0),
        name="place",
    )(near, far)


def plane_groups():
    return [[(side * RING + ring) * SLABS + slab for side in range(2) for slab in range(SLABS)] for ring in range(RING)]


def core_groups():
    return [
        [(side * RING + ring) * SLABS + 2 * chip + core for side in range(2) for chip in range(SLABS // 2)]
        for ring in range(RING)
        for core in range(2)
    ]


def ring_pairs(even, odd):
    pairs = []
    for side in range(2):
        for ring in range(RING):
            for slab in range(SLABS):
                step = odd if slab % 2 else even
                pairs.append(((side * RING + ring) * SLABS + slab, (side * RING + (ring + step) % RING) * SLABS + slab))
    return pairs


def side_pairs():
    return [(place, place ^ (RING * SLABS)) for place in range(2 * RING * SLABS)]


def core_pairs():
    return [(place, place ^ 1) for place in range(2 * RING * SLABS)]


def over_plane(block):
    return lax.all_to_all(block, BOTH, 0, 0, axis_index_groups=plane_groups(), tiled=True)


def by_depth(block):
    return block.reshape(PEERS * OWN, DEPTH, HALF).transpose(1, 0, 2)


def after(value, *earlier):
    return lax.optimization_barrier((value, *earlier))[0]


def on_device(orbitals, potential):
    block = orbitals.reshape(SLABS, OWN, DEPTH, PLANE)
    shared = jnp.broadcast_to(potential[None, None], (SLABS, 1, DEPTH, PLANE))
    block = lax.all_to_all(jnp.concatenate([block, shared], axis=1), "slab", 0, 0, tiled=True)
    filtered_low, filtered_rest, applied = run_filter(block)
    own_low = by_depth(over_plane(filtered_low))
    ahead = lax.ppermute(own_low, BOTH, ring_pairs(1, 1))
    behind = lax.ppermute(own_low, BOTH, ring_pairs(-1, -1))
    blocks = [ahead, behind]
    filtered_rest = over_plane(filtered_rest)
    ahead, applied = lax.optimization_barrier((ahead, applied))
    behind, applied = lax.optimization_barrier((behind, applied))
    ahead = lax.ppermute(ahead, BOTH, ring_pairs(1, 1))
    behind = lax.ppermute(behind, BOTH, ring_pairs(-1, -1))
    blocks += [ahead, behind]
    ahead, filtered_rest = lax.optimization_barrier((ahead, filtered_rest))
    behind, filtered_rest = lax.optimization_barrier((behind, filtered_rest))
    applied = over_plane(applied)
    ahead = lax.ppermute(ahead, BOTH, ring_pairs(1, 1))
    behind = lax.ppermute(behind, BOTH, ring_pairs(-1, -1))
    blocks += [ahead, behind]
    ahead, applied = lax.optimization_barrier((ahead, applied))
    behind, applied = lax.optimization_barrier((behind, applied))
    last = jnp.where(lax.axis_index("slab") % 2 == 0, ahead, behind)
    last = lax.ppermute(last, BOTH, ring_pairs(1, -1))
    weights, keep, send = run_early(own_low, by_depth(applied[:, :OWN]), by_depth(applied[:, OWN:]), blocks)
    near, far = run_join(own_low, filtered_rest)
    far = lax.ppermute(far, BOTH, side_pairs())
    filtered = run_place(near, after(far, keep))
    last, filtered = lax.optimization_barrier((last, filtered))
    keep, send = run_late(weights, last, keep, send)
    sums = (keep + lax.ppermute(send, BOTH, core_pairs()))[: 2 * RING]
    sums = lax.all_to_all(sums, BOTH, 0, 0, axis_index_groups=core_groups(), tiled=True)
    sums = jnp.sum(sums, axis=0) / NCELLS
    return filtered.reshape(SLABS * OWN, DEPTH, PLANE), sums[:, :64], sums[:, 64:]


def solution(mesh):
    return jax.shard_map(
        on_device,
        mesh=mesh,
        in_specs=(P("band", "slab", None), P("slab", None)),
        out_specs=(P("band", "slab", None), P("band", "slab"), P("band", "slab")),
        check_vma=False,
    )
```

```python
import jax
import jax.numpy as jnp
import numpy as np
from jax import lax
from jax.experimental import pallas as pl
from jax.experimental.pallas import tpu as pltpu
from jax.sharding import PartitionSpec as P

DEGREE = 4
NY = 16
NX = 32
NZ = 128
PLANE = NX * NY
NCELLS = NZ * PLANE
SLABS = 16
DEPTH = NZ // SLABS
OWN = 4
HALF = PLANE // 2
RING = 8
PEERS = 32

COEFFS = (
    -5369.0 / 1800.0,
    12.0 / 7.0,
    -15.0 / 56.0,
    10.0 / 189.0,
    -1.0 / 112.0,
    2.0 / 1925.0,
    -1.0 / 16632.0,
)
SPACING = 0.6
LOWER = -2.0
CUTOFF = 8.0
UPPER = 32.0
KINETIC = -0.5 / SPACING**2
DIAGONAL = 3.0 * COEFFS[0] * KINETIC
BF16 = jnp.bfloat16
F32 = jnp.float32
BOTH = ("band", "slab")
KERNEL_BYTES = 16 * 1024 * 1024


def line_matrix(size):
    matrix = np.zeros((size, size))
    for reach in range(1, 7):
        matrix += KINETIC * COEFFS[reach] * (np.eye(size, k=reach) + np.eye(size, k=-reach))
    return matrix


def two_terms(matrix):
    high = matrix.astype(jnp.bfloat16)
    low = (matrix - high.astype(np.float64)).astype(jnp.bfloat16)
    return high, low


def stencil_matrices():
    plane = np.kron(line_matrix(NX), np.eye(NY)) + np.kron(np.eye(NX), line_matrix(NY))
    plane_high, plane_low = two_terms(plane)
    z_high, z_low = two_terms(line_matrix(NZ))
    return plane_high, plane_low, np.concatenate([z_high, z_low, z_high], axis=1)


def schedule():
    half_width = (UPPER - CUTOFF) / 2.0
    center = (UPPER + CUTOFF) / 2.0
    sigma_first = half_width / (LOWER - center)
    sigma = sigma_first
    steps = [(sigma_first / half_width, center, 0.0)]
    for _ in range(DEGREE - 1):
        sigma_next = 1.0 / (2.0 / sigma_first - sigma)
        steps.append((2.0 * sigma_next / half_width, center, sigma * sigma_next))
        sigma = sigma_next
    return steps


def slab_rows(slab):
    return slice(slab * DEPTH, (slab + 1) * DEPTH)


def put_low(ref, orb, value):
    for slab in range(SLABS):
        for side in range(2):
            ref[side * SLABS + slab, orb] = value[slab_rows(slab), side * HALF : (side + 1) * HALF].astype(BF16)


def pack_kernel(orbitals_ref, potential_ref, out_ref, done):
    copies = [pltpu.make_async_copy(orbitals_ref, out_ref.at[:, :OWN], done.at[SLABS])]
    copies += [pltpu.make_async_copy(potential_ref, out_ref.at[slab, OWN], done.at[slab]) for slab in range(SLABS)]
    for copy in copies:
        copy.start()
    for copy in copies:
        copy.wait()


def run_pack(orbitals, potential):
    return pl.pallas_call(
        pack_kernel,
        out_shape=jax.ShapeDtypeStruct((SLABS, OWN + 1, DEPTH, PLANE), F32),
        in_specs=[pl.BlockSpec(memory_space=pltpu.HBM)] * 2,
        out_specs=pl.BlockSpec(memory_space=pltpu.VMEM),
        scratch_shapes=[pltpu.SemaphoreType.DMA((SLABS + 1,))],
        compiler_params=pltpu.CompilerParams(vmem_limit_bytes=KERNEL_BYTES),
        name="pack",
    )(orbitals, potential)


def filter_kernel(x_ref, mh_ref, ml_ref, z_ref, out_ref, low_ref, rest_ref, field_a, field_b, pot, split, total):
    for slab in range(SLABS):
        for orb in range(OWN):
            field_a[orb, slab_rows(slab), :] = x_ref[slab, orb]
        pot[slab_rows(slab), :] = x_ref[slab, OWN] + DIAGONAL

    current, previous = field_a, field_b
    steps = schedule()
    for number, (scale, center, back) in enumerate(steps):
        for orb in range(OWN):
            rows = slice(orb * NZ, (orb + 1) * NZ)
            value = current[orb]
            high = value.astype(BF16)
            split[0, rows, :] = high
            split[1, rows, :] = (value - high.astype(F32)).astype(BF16)
        total[...] = (
            jnp.dot(split[0], mh_ref[...], preferred_element_type=F32)
            + jnp.dot(split[0], ml_ref[...], preferred_element_type=F32)
            + jnp.dot(split[1], mh_ref[...], preferred_element_type=F32)
        )
        for orb in range(OWN):
            rows = slice(orb * NZ, (orb + 1) * NZ)
            stack = jnp.concatenate([split[0, rows, :], split[0, rows, :], split[1, rows, :]], axis=0)
            applied = total[rows, :] + jnp.dot(z_ref[...], stack, preferred_element_type=F32)
            following = scale * (applied + (pot[...] - center) * current[orb])
            if number:
                following = following - back * previous[orb]
            previous[orb] = following
            if number == len(steps) - 1:
                high = following.astype(BF16).astype(F32)
                put_low(low_ref, orb, high)
                put_low(rest_ref, orb, following - high)
                for slab in range(SLABS):
                    out_ref[slab, orb] = following[slab_rows(slab), :]
        current, previous = previous, current


def apply_kernel(x_ref, f_ref, mh_ref, ml_ref, z_ref, app_ref, pot, split, total, rest):
    for slab in range(SLABS):
        for orb in range(OWN):
            rows = slice(orb * NZ + slab * DEPTH, orb * NZ + (slab + 1) * DEPTH)
            total[rows, :] = f_ref[slab, orb]
        pot[slab_rows(slab), :] = x_ref[slab, OWN] + DIAGONAL
    for orb in range(OWN):
        rows = slice(orb * NZ, (orb + 1) * NZ)
        value = total[rows, :]
        high = value.astype(BF16)
        split[0, rows, :] = high
        split[1, rows, :] = (value - high.astype(F32)).astype(BF16)
    total[...] = jnp.dot(split[0], mh_ref[...], preferred_element_type=F32) + jnp.dot(
        split[0], ml_ref[...], preferred_element_type=F32
    )
    rest[...] = jnp.dot(split[1], mh_ref[...], preferred_element_type=F32)
    for orb in range(OWN):
        rows = slice(orb * NZ, (orb + 1) * NZ)
        high, low = split[0, rows, :], split[1, rows, :]
        stack = jnp.concatenate([high, high], axis=0)
        of_low = total[rows, :] + pot[...] * high.astype(F32)
        of_low = of_low + jnp.dot(z_ref[:, : 2 * NZ], stack, preferred_element_type=F32)
        of_rest = rest[rows, :] + pot[...] * low.astype(F32)
        of_rest = of_rest + jnp.dot(z_ref[:, 2 * NZ :], low, preferred_element_type=F32)
        applied_low = (of_low + of_rest).astype(BF16).astype(F32)
        middle = 0.5 * (applied_low + of_low)
        middle_high = middle.astype(BF16).astype(F32)
        put_low(app_ref, orb, middle_high)
        put_low(app_ref, OWN + orb, middle - middle_high)


def run_filter(block):
    plane_high, plane_low, z_stack = (jnp.asarray(matrix) for matrix in stencil_matrices())
    vmem = pl.BlockSpec(memory_space=pltpu.VMEM)
    params = pltpu.CompilerParams(vmem_limit_bytes=KERNEL_BYTES)
    filtered, filtered_low, filtered_rest = pl.pallas_call(
        filter_kernel,
        out_shape=(
            jax.ShapeDtypeStruct((SLABS, OWN, DEPTH, PLANE), F32),
            jax.ShapeDtypeStruct((PEERS, OWN, DEPTH, HALF), BF16),
            jax.ShapeDtypeStruct((PEERS, OWN, DEPTH, HALF), BF16),
        ),
        in_specs=[vmem] * 4,
        out_specs=(vmem, vmem, vmem),
        scratch_shapes=[
            pltpu.VMEM((OWN, NZ, PLANE), F32),
            pltpu.VMEM((OWN, NZ, PLANE), F32),
            pltpu.VMEM((NZ, PLANE), F32),
            pltpu.VMEM((2, OWN * NZ, PLANE), BF16),
            pltpu.VMEM((OWN * NZ, PLANE), F32),
        ],
        compiler_params=params,
        cost_estimate=pl.CostEstimate(flops=5_000_000_000, bytes_accessed=6_000_000, transcendentals=0),
        name="chebyshev",
    )(block, plane_high, plane_low, z_stack)
    applied = pl.pallas_call(
        apply_kernel,
        out_shape=jax.ShapeDtypeStruct((PEERS, 2 * OWN, DEPTH, HALF), BF16),
        in_specs=[vmem] * 5,
        out_specs=vmem,
        scratch_shapes=[
            pltpu.VMEM((NZ, PLANE), F32),
            pltpu.VMEM((2, OWN * NZ, PLANE), BF16),
            pltpu.VMEM((OWN * NZ, PLANE), F32),
            pltpu.VMEM((OWN * NZ, PLANE), F32),
        ],
        compiler_params=params,
        cost_estimate=pl.CostEstimate(flops=1_000_000_000, bytes_accessed=6_000_000, transcendentals=0),
        name="applied",
    )(block, filtered, plane_high, plane_low, z_stack)
    return filtered_low, filtered_rest, applied


def put_pairs(total, shift, keep_ref, send_ref):
    place = lax.rem(lax.axis_index("band"), RING)
    core = lax.rem(lax.axis_index("slab"), 2)
    ring = lax.rem(place + shift + RING, RING)
    mine = lax.rem(ring, 2) == core
    for own in range(2):
        rows = total[own * 192 : (own + 1) * 192]
        gram, cross = rows[:64], rows[64:128] + rows[128:]
        for side in range(2):
            lanes = slice(side * 64, (side + 1) * 64)
            block = jnp.concatenate([gram[:, lanes], cross[:, lanes]], axis=1)
            index = own * RING + side * (RING // 2) + lax.div(ring, 2)
            keep_ref[jnp.where(mine, index, 2 * RING)] = block
            send_ref[jnp.where(mine, 2 * RING, index)] = block


def pair_sum(w_ref, pick):
    total = None
    for depth in range(DEPTH):
        part = lax.dot_general(w_ref[depth], pick(depth), (((1,), (1,)), ((), ())), preferred_element_type=F32)
        total = part if total is None else total + part
    return total


def early_kernel(own_ref, high_ref, rest_ref, *refs):
    blocks, (w_ref, keep_ref, send_ref) = refs[:-3], refs[-3:]
    for side in range(2):
        for place, ref in enumerate((own_ref, high_ref, rest_ref)):
            start = side * 192 + place * 64
            w_ref[:, start : start + 64, :] = ref[:, side * 64 : (side + 1) * 64, :]
    put_pairs(pair_sum(w_ref, lambda depth: own_ref[depth]), 0, keep_ref, send_ref)
    for step in range(1, RING // 2):
        ahead, behind = blocks[2 * step - 2], blocks[2 * step - 1]
        total = pair_sum(w_ref, lambda depth: jnp.concatenate([ahead[depth], behind[depth]], axis=0))
        put_pairs(total[:, :128], -step, keep_ref, send_ref)
        put_pairs(total[:, 128:], step, keep_ref, send_ref)


def late_kernel(w_ref, last_ref, keep_in, send_in, keep_ref, send_ref):
    put_pairs(pair_sum(w_ref, lambda depth: last_ref[depth]), RING // 2, keep_ref, send_ref)


def run_early(own_low, high, rest, blocks):
    vmem = pl.BlockSpec(memory_space=pltpu.VMEM)
    shape = jax.ShapeDtypeStruct((2 * RING + 1, 64, 128), F32)
    return pl.pallas_call(
        early_kernel,
        out_shape=(jax.ShapeDtypeStruct((DEPTH, 6 * 64, HALF), BF16), shape, shape),
        in_specs=[vmem] * (3 + len(blocks)),
        out_specs=(vmem, vmem, vmem),
        compiler_params=pltpu.CompilerParams(vmem_limit_bytes=KERNEL_BYTES),
        cost_estimate=pl.CostEstimate(flops=1_400_000_000, bytes_accessed=6_000_000, transcendentals=0),
        name="pairs_early",
    )(own_low, high, rest, *blocks)


def run_late(weights, last, keep, send):
    vmem = pl.BlockSpec(memory_space=pltpu.VMEM)
    shape = jax.ShapeDtypeStruct(keep.shape, F32)
    return pl.pallas_call(
        late_kernel,
        out_shape=(shape, shape),
        in_specs=[vmem] * 4,
        out_specs=(vmem, vmem),
        input_output_aliases={2: 0, 3: 1},
        compiler_params=pltpu.CompilerParams(vmem_limit_bytes=KERNEL_BYTES),
        cost_estimate=pl.CostEstimate(flops=200_000_000, bytes_accessed=2_000_000, transcendentals=0),
        name="pairs_late",
    )(weights, last, keep, send)


def join_kernel(own_ref, rest_ref, near_ref, far_ref):
    side = lax.div(lax.axis_index("band"), RING)
    for ref, which in ((near_ref, side), (far_ref, 1 - side)):
        rows = pl.ds(pl.multiple_of(which * 64, 64), 64)
        high = jnp.swapaxes(own_ref[:, rows, :].astype(F32), 0, 1).reshape(SLABS, OWN, DEPTH, HALF)
        ref[...] = high + rest_ref[pl.ds(which * SLABS, SLABS)].astype(F32)


def run_join(own_low, rest):
    vmem = pl.BlockSpec(memory_space=pltpu.VMEM)
    shape = jax.ShapeDtypeStruct((SLABS, OWN, DEPTH, HALF), F32)
    return pl.pallas_call(
        join_kernel,
        out_shape=(shape, shape),
        in_specs=[vmem, vmem],
        out_specs=(vmem, vmem),
        compiler_params=pltpu.CompilerParams(vmem_limit_bytes=KERNEL_BYTES),
        cost_estimate=pl.CostEstimate(flops=1_000_000, bytes_accessed=2_000_000, transcendentals=0),
        name="join",
    )(own_low, rest)


def place_kernel(near_ref, far_ref, out_ref, done):
    side = lax.div(lax.axis_index("band"), RING)
    copies = []
    for number, (ref, which) in enumerate(((near_ref, side), (far_ref, 1 - side))):
        lanes = pl.ds(pl.multiple_of(which * HALF, HALF), HALF)
        copies.append(pltpu.make_async_copy(ref, out_ref.at[:, :, :, lanes], done.at[number]))
    for copy in copies:
        copy.start()
    for copy in copies:
        copy.wait()


def run_place(near, far):
    vmem = pl.BlockSpec(memory_space=pltpu.VMEM)
    return pl.pallas_call(
        place_kernel,
        out_shape=jax.ShapeDtypeStruct((SLABS, OWN, DEPTH, PLANE), F32),
        in_specs=[vmem, vmem],
        out_specs=pl.BlockSpec(memory_space=pl.ANY),
        scratch_shapes=[pltpu.SemaphoreType.DMA((2,))],
        compiler_params=pltpu.CompilerParams(vmem_limit_bytes=KERNEL_BYTES),
        cost_estimate=pl.CostEstimate(flops=0, bytes_accessed=2_000_000, transcendentals=0),
        name="place",
    )(near, far)


def plane_groups():
    return [[(side * RING + ring) * SLABS + slab for side in range(2) for slab in range(SLABS)] for ring in range(RING)]


def core_groups():
    return [
        [(side * RING + ring) * SLABS + 2 * chip + core for side in range(2) for chip in range(SLABS // 2)]
        for ring in range(RING)
        for core in range(2)
    ]


def ring_pairs(even, odd):
    pairs = []
    for side in range(2):
        for ring in range(RING):
            for slab in range(SLABS):
                step = odd if slab % 2 else even
                pairs.append(((side * RING + ring) * SLABS + slab, (side * RING + (ring + step) % RING) * SLABS + slab))
    return pairs


def side_pairs():
    return [(place, place ^ (RING * SLABS)) for place in range(2 * RING * SLABS)]


def core_pairs():
    return [(place, place ^ 1) for place in range(2 * RING * SLABS)]


def over_plane(block):
    return lax.all_to_all(block, BOTH, 0, 0, axis_index_groups=plane_groups(), tiled=True)


def by_depth(block):
    return block.reshape(PEERS * OWN, DEPTH, HALF).transpose(1, 0, 2)


def after(value, *earlier):
    return lax.optimization_barrier((value, *earlier))[0]


def on_device(orbitals, potential):
    block = run_pack(orbitals.reshape(SLABS, OWN, DEPTH, PLANE), potential)
    block = lax.all_to_all(block, "slab", 0, 0, tiled=True)
    filtered_low, filtered_rest, applied = run_filter(block)
    own_low = by_depth(over_plane(filtered_low))
    ahead = lax.ppermute(own_low, BOTH, ring_pairs(1, 1))
    behind = lax.ppermute(own_low, BOTH, ring_pairs(-1, -1))
    blocks = [ahead, behind]
    filtered_rest = over_plane(filtered_rest)
    ahead, applied = lax.optimization_barrier((ahead, applied))
    behind, applied = lax.optimization_barrier((behind, applied))
    ahead = lax.ppermute(ahead, BOTH, ring_pairs(1, 1))
    behind = lax.ppermute(behind, BOTH, ring_pairs(-1, -1))
    blocks += [ahead, behind]
    ahead, filtered_rest = lax.optimization_barrier((ahead, filtered_rest))
    behind, filtered_rest = lax.optimization_barrier((behind, filtered_rest))
    applied = over_plane(applied)
    ahead = lax.ppermute(ahead, BOTH, ring_pairs(1, 1))
    behind = lax.ppermute(behind, BOTH, ring_pairs(-1, -1))
    blocks += [ahead, behind]
    ahead, applied = lax.optimization_barrier((ahead, applied))
    behind, applied = lax.optimization_barrier((behind, applied))
    last = jnp.where(lax.axis_index("slab") % 2 == 0, ahead, behind)
    last = lax.ppermute(last, BOTH, ring_pairs(1, -1))
    weights, keep, send = run_early(own_low, by_depth(applied[:, :OWN]), by_depth(applied[:, OWN:]), blocks)
    near, far = run_join(own_low, filtered_rest)
    far = lax.ppermute(far, BOTH, side_pairs())
    filtered = run_place(near, after(far, keep))
    last, filtered = lax.optimization_barrier((last, filtered))
    keep, send = run_late(weights, last, keep, send)
    sums = (keep + lax.ppermute(send, BOTH, core_pairs()))[: 2 * RING]
    sums = lax.all_to_all(sums, BOTH, 0, 0, axis_index_groups=core_groups(), tiled=True)
    sums = jnp.sum(sums, axis=0) / NCELLS
    return filtered.reshape(SLABS * OWN, DEPTH, PLANE), sums[:, :64], sums[:, 64:]


def solution(mesh):
    return jax.shard_map(
        on_device,
        mesh=mesh,
        in_specs=(P("band", "slab", None), P("slab", None)),
        out_specs=(P("band", "slab", None), P("band", "slab"), P("band", "slab")),
        check_vma=False,
    )
```
